128 devices in a mesh: attn: 16 (over y, z), expert: 8 (over x, core).
Axes of the slice: x: 4, y: 4, z: 4, core: 2. Of those that a mesh axis runs over, the one named last changes fastest.
Arguments:
- resid: bfloat16 [1024, 6144], P('attn')
- queries: bfloat16 [1024, 3072], P('attn', 'expert')
- new_keys: bfloat16 [1024, 1024], P('attn', 'expert'), may hold values from -6 to 6
- new_values: bfloat16 [1024, 1024], P('attn', 'expert'), may hold values from -12 to 12
- cache_k: bfloat16 [1024, 256, 1024], P('attn', None, 'expert')
- cache_v: bfloat16 [1024, 256, 1024], P('attn', None, 'expert'), may hold values from -12 to 12
- lengths: int32 [1024], P('attn'), may hold values from 2 to 256, as said below
- out_proj: bfloat16 [3072, 6144], P('expert'), may hold values from -0.109375 to 0.109375
- norm_gain: bfloat16 [6144], replicated, may hold values from 0.099609375 to 1.8984375
- router: bfloat16 [6144, 8], replicated, may hold values from -0.078125 to 0.078125
- route_ids: int32 [1024, 2], P('attn'), may hold values from 0 to 7, all different within a row; in each aligned block of 32 rows (0 to 31, 32 to 63, ...) at most 16 rows name the same one
- w_gate: bfloat16 [8, 6144, 8192], P('expert', None, 'attn'), may hold values from -0.078125 to 0.078125
- w_up: bfloat16 [8, 6144, 8192], P('expert', None, 'attn'), may hold values from -0.078125 to 0.078125
- w_down: bfloat16 [8, 8192, 6144], P('expert', 'attn'), may hold values from -0.0625 to 0.0625
Outputs:
- layer_out: bfloat16 [1024, 6144], P('attn', 'expert')
The draws below stay inside these ranges and needn't reach their ends.
Inputs may be any that keep to these rules, and one draw needn't show every extreme that they name: `route_ids`: each row names two different experts. Within each aligned block of 32 rows (one micro-batch of one attention index) no expert is named by more than 16 rows, and some expert reaches 16 in some blocks. `lengths`: the first row of each attention index uses all 256 positions.
All inputs are finite; a program needn't handle non-finite values.
Results may differ from the reference program's by a relative error of at most 0.023.
Values may be sent and summed in bfloat16 or wider, within the bound.
No kernel may reach another device: no remote copies, remote signals or barrier semaphores. Data moves between devices by JAX's collectives and lax.ppermute only.
A program may use at most 192 MiB of HBM per device.

```python
import math
import jax
import jax.numpy as jnp
import numpy as np
from jax import lax

D = 6144
HD = 128
KVH = 8
QH = 24
EXPERTS = 8
FFW = 8192
TOP = 2
MICRO = 2
MB = 32
L = 256
MOST = 16
ROWS = 1024
N_ATTN = 16


def shared_keys(key):
    return jax.random.normal(key, (ROWS, L, KVH * HD), jnp.float32)


def draw_cache_k(key, part):
    base = shared_keys(key)
    return base.astype(jnp.bfloat16)


def draw_queries(key, part):
    key = jax.random.fold_in(key, 23)
    first_key = jax.random.fold_in(key, 0)
    values = jax.random.normal(first_key, (ROWS, QH * HD), jnp.float32)
    return values.astype(jnp.bfloat16)


def draw_resid(key, part):
    key = jax.random.fold_in(key, 5)
    core_key, column_key, row_key = jax.random.split(key, 3)
    position = jnp.arange(D, dtype=jnp.float32)[None, :] / D
    column_scale = jnp.power(10.0, 0.5 * jax.random.uniform(column_key, (1, D), jnp.float32) + 0.5 * position - 1.0)
    row_scale = jnp.power(10.0, jax.random.uniform(row_key, (ROWS, 1), jnp.float32) - 0.5)
    core = jax.random.normal(core_key, (ROWS, D), jnp.float32)
    return (core * column_scale * row_scale).astype(jnp.bfloat16)


def draw_lengths(key, part):
    key = jax.random.fold_in(key, 31)
    values = jax.random.randint(key, (ROWS,), 2, L + 1)
    leading = jnp.arange(ROWS) % (MICRO * MB) == 0
    return jnp.where(leading, L, values).astype(jnp.int32)


def level_of(rng, dims, cuts, smallest, high):
    level = 1.0
    for dim, blocks in cuts:
        draws = jax.random.uniform(jax.random.fold_in(jax.random.fold_in(rng, 6), dim), (blocks,), jnp.float32, smallest / len(cuts), high / len(cuts))
        level = level * jnp.repeat(jnp.exp(draws), dims[dim] // blocks).reshape((-1,) + (1,) * (len(dims) - 1 - dim))
    return level


def deal_out(key, own, number, rows, number_of, top, bound, slope):
    ranking = jax.random.permutation(key, number_of)
    heavy_load, ordinary = portions_of(number_of, rows * top, bound, slope, True), portions_of(number_of, rows * top, bound, slope, False)
    places = jnp.arange(number_of)

    def named(tallies, turn):
        used = int((tallies > 0).sum())
        fixed = max(1, used // 4)
        moved = fixed + (places - fixed + turn * (used - fixed)) % max(1, number_of - fixed)
        return jnp.zeros((number_of,), jnp.int32).at[ranking[jnp.where(places < fixed, places, moved)]].set(jnp.asarray(tallies, jnp.int32))

    tallies = jnp.where(number % 4 == 0, named(heavy_load, number // 4), named(ordinary, number - number // 4 - 1))
    mixed = jax.random.permutation(jax.random.fold_in(own, 3), number_of)
    source_of, receiver = mixed[0:number_of // 2 * 2:2], mixed[1:number_of // 2 * 2:2]
    room = jnp.minimum(tallies[source_of] - 1, bound - tallies[receiver]) // 2
    room = jnp.where((source_of == ranking[0]) | (receiver == ranking[0]) | (tallies[receiver] == 0), 0, jnp.maximum(room, 0))
    moved = jax.random.randint(jax.random.fold_in(own, 4), (number_of // 2,), 0, 1 << 20) % (room + 1)
    tallies = tallies.at[source_of].add(-moved).at[receiver].add(moved)
    labels = jnp.searchsorted(jnp.cumsum(tallies), jnp.arange(rows * top), side="right").astype(jnp.int32)
    grid = labels.reshape(top, rows).T
    grid = grid[jax.random.permutation(jax.random.fold_in(own, 1), rows)]
    turn = jax.random.randint(jax.random.fold_in(own, 2), (rows, 1), 0, top)
    return jnp.take_along_axis(grid, (jnp.arange(top)[None, :] + turn) % top, axis=1)


def portions_of(amount, total, limit, slope, full):
    portions = [(1 << 20) // math.isqrt(grade ** slope) + 1 for grade in range(1, amount + 1)]
    largest = limit if full else min(limit, max(-(-total // amount), total * portions[0] // sum(portions)))
    least = 1 if total - largest >= amount - 1 else 0
    counts, surplus = [largest] + [least] * (amount - 1), total - largest - least * (amount - 1)
    while surplus > 0:
        movable = [i for i in range(1, amount) if counts[i] < largest] or [i for i in range(1, amount) if counts[i] < limit]
        mass, budget = sum([portions[i] for i in movable]), surplus
        for i in movable:
            more = min(limit - counts[i], max(1, budget * portions[i] // mass), surplus)
            counts[i] = counts[i] + more
            surplus = surplus - more
    return np.array(counts)


def centred(own_key, dims, scale, bound, cuts=(), held_as=jnp.bfloat16):
    entries = scale * jax.random.normal(own_key, dims, jnp.float32)
    if cuts:
        entries = entries * level_of(own_key, dims, cuts, -0.22, 0.18)
    return jnp.clip(entries, -bound, bound).astype(held_as)


def setup_inputs(seed: int = 0) -> dict:
    seeds = jax.random.split(jax.random.key(seed), 15)
    resid = draw_resid(jax.random.fold_in(seeds[14], 71), 0)
    queries = draw_queries(jax.random.fold_in(seeds[14], 71), 0)
    new_keys = centred(seeds[2], (ROWS, KVH * HD), 1.0, 6.0, ((0, 16), (1, 8)))
    new_values = centred(seeds[3], (ROWS, KVH * HD), 2.0, 12.0, ((0, 16), (1, 8)))
    cache_k = draw_cache_k(jax.random.fold_in(seeds[14], 71), 0)
    cache_v = centred(seeds[5], (ROWS, L, KVH * HD), 2.0, 12.0, ((0, 16), (2, 8)))
    lengths = draw_lengths(jax.random.fold_in(seeds[14], 71), 0)
    out_proj = centred(seeds[7], (QH * HD, D), (QH * HD) ** -0.5, 0.109375, ((0, 8),))
    norm_gain = jnp.clip(1.0 + 0.18 * jax.random.normal(seeds[8], (D,), jnp.float32), 0.099609375, 1.8984375).astype(jnp.bfloat16)
    router = centred(seeds[9], (D, EXPERTS), D ** -0.5, 0.078125)
    route_ids_keys = jax.random.split(jax.random.fold_in(seeds[10], 1), ROWS // MB)
    route_ids_turns = jax.random.permutation(jax.random.fold_in(seeds[10], 3), ROWS // MB)
    route_ids = jax.vmap(lambda own, number: deal_out(jax.random.fold_in(seeds[10], 2), own, number, MB, EXPERTS, 2, MOST, 2))(route_ids_keys, route_ids_turns).reshape((ROWS, TOP))
    w_gate = centred(seeds[11], (EXPERTS, D, FFW), D ** -0.5, 0.078125, ((0, 8), (2, 16)))
    w_up = centred(seeds[12], (EXPERTS, D, FFW), D ** -0.5, 0.078125, ((0, 8), (2, 16)))
    w_down = centred(seeds[13], (EXPERTS, FFW, D), FFW ** -0.5, 0.0625, ((0, 8), (1, 16)))
    return dict(resid=resid, queries=queries, new_keys=new_keys, new_values=new_values, cache_k=cache_k, cache_v=cache_v, lengths=lengths, out_proj=out_proj, norm_gain=norm_gain, router=router, route_ids=route_ids, w_gate=w_gate, w_up=w_up, w_down=w_down)


def attend(queries, new_keys, new_values, cache_k, cache_v, lengths, kv_heads):
    count = queries.shape[0]
    length = cache_k.shape[1]
    group = queries.shape[1] // (kv_heads * HD)
    query = queries.astype(jnp.float32).reshape(count, kv_heads, group, HD)
    keys = cache_k.astype(jnp.float32).reshape(count, length, kv_heads, HD)
    values = cache_v.astype(jnp.float32).reshape(count, length, kv_heads, HD)
    fresh_key = new_keys.astype(jnp.float32).reshape(count, kv_heads, HD)
    fresh_value = new_values.astype(jnp.float32).reshape(count, kv_heads, HD)
    factor = 1.0 / math.sqrt(HD)
    scores = jnp.einsum('rjhd,rljd->rjhl', query, keys) * factor
    itself = jnp.einsum('rjhd,rjd->rjh', query, fresh_key) * factor
    valid = (jnp.arange(length)[None, :] < lengths[:, None])[:, None, None, :]
    masked = jnp.where(valid, scores, -jnp.inf)
    highest = jnp.maximum(lax.optimization_barrier(jnp.max(masked, axis=-1)), itself)
    spread = jnp.exp(masked - highest[..., None])
    own_exp = jnp.exp(itself - highest)
    total = lax.optimization_barrier(jnp.sum(spread, axis=-1)) + own_exp
    weights = (spread / total[..., None]).astype(jnp.bfloat16)
    own_weight = (own_exp / total).astype(jnp.bfloat16)
    mixed = jnp.einsum('rjhl,rljd->rjhd', weights.astype(jnp.float32), values)
    mixed = mixed + own_weight.astype(jnp.float32)[..., None] * fresh_value[:, :, None, :]
    return mixed.reshape(count, -1).astype(jnp.bfloat16)

def slot_numbers(routes, experts):
    blocks, size, top_count = routes.shape
    onehot = (routes[..., None] == jnp.arange(experts, dtype=jnp.int32)[None, None, None, :]).astype(jnp.int32)
    flat = onehot.reshape(blocks, size * top_count, experts)
    before = jnp.cumsum(flat, axis=1) - flat
    return lax.optimization_barrier(jnp.sum(before * flat, axis=-1)).reshape(blocks, size, top_count)

def reference(resid, queries, new_keys, new_values, cache_k, cache_v, lengths, out_proj, norm_gain, router, route_ids, w_gate, w_up, w_down):
    heads_out = attend(queries, new_keys, new_values, cache_k, cache_v, lengths, KVH)
    state = resid.astype(jnp.float32) + jnp.dot(heads_out, out_proj, preferred_element_type=jnp.float32)
    mean_square = lax.optimization_barrier(jnp.mean(state * state, axis=1, keepdims=True))
    normed = (state * lax.rsqrt(mean_square + 1e-05) * norm_gain.astype(jnp.float32)[None, :]).astype(jnp.bfloat16)
    logits = jnp.dot(normed, router, preferred_element_type=jnp.float32)
    match = route_ids[:, :, None] == jnp.arange(EXPERTS, dtype=jnp.int32)[None, None, :]
    chosen = lax.optimization_barrier(jnp.sum(jnp.where(match, logits[:, None, :], 0.0), axis=-1))
    gates = jax.nn.softmax(chosen, axis=-1).astype(jnp.bfloat16)
    blocks = ROWS // MB
    routes = route_ids.reshape(blocks, MB, TOP)
    slots = slot_numbers(routes, EXPERTS)
    normed_blocks = normed.reshape(blocks, MB, D).astype(jnp.float32)
    gate_blocks = gates.astype(jnp.float32).reshape(blocks, MB, TOP)
    width = FFW // N_ATTN

    def one_expert(expert):
        placed = (routes == expert)[..., None] & (slots[..., None] == jnp.arange(MOST, dtype=jnp.int32)[None, None, None, :])
        dispatch = lax.optimization_barrier(jnp.sum(placed.astype(jnp.float32), axis=2))
        combine = lax.optimization_barrier(jnp.sum(jnp.where(placed, gate_blocks[..., None], 0.0), axis=2))
        sectioned = jnp.einsum('nms,nmd->nsd', dispatch, normed_blocks).astype(jnp.bfloat16).reshape(blocks * MOST, D)
        gate = jnp.dot(sectioned, w_gate[expert], preferred_element_type=jnp.float32)
        upper = jnp.dot(sectioned, w_up[expert], preferred_element_type=jnp.float32)
        expanded = (jax.nn.silu(gate) * upper).astype(jnp.bfloat16)
        pieces = expanded.astype(jnp.float32).reshape(blocks * MOST, N_ATTN, width)
        down_full = w_down[expert].astype(jnp.float32).reshape(N_ATTN, width, D)
        parts = jnp.einsum('san,and->sad', pieces, down_full)
        rounded = lax.optimization_barrier(parts.astype(jnp.bfloat16)).astype(jnp.float32)
        expert_out = lax.optimization_barrier(jnp.sum(rounded, axis=1)).reshape(blocks, MOST, D)
        return jnp.einsum('nms,nsd->nmd', combine, expert_out, precision=lax.Precision.HIGHEST)
    terms = lax.map(one_expert, jnp.arange(EXPERTS, dtype=jnp.int32))
    moe = lax.optimization_barrier(jnp.sum(terms, axis=0)).reshape(ROWS, D)
    return (state + moe).astype(jnp.bfloat16)
```

```python
import math

import jax
import jax.numpy as jnp
from jax import lax
from jax.sharding import Mesh
from jax.sharding import PartitionSpec as P

HD = 128
TOP = 2
MICRO = 2
MB = 32
SIDE = 4
EXPERT_AXES = ("x", "c")

epsilon = 1e-05


def shift(value, axis, step):
    return lax.ppermute(value, axis, [(i, (i + step) % SIDE) for i in range(SIDE)])


def ring(value, axis):
    perm = []
    for i in range(SIDE):
        perm.append((2 * i, 2 * ((i + 1) % SIDE)))
        perm.append((2 * i + 1, 2 * ((i - 1) % SIDE) + 1))
    return lax.ppermute(value, (axis, "c"), perm)


def attend(queries, new_keys, new_values, cache_k, cache_v, lengths):
    count = queries.shape[0]
    length = cache_k.shape[1]
    group = queries.shape[1] // HD
    query = queries.reshape(count, group, HD)
    factor = 1.0 / math.sqrt(HD)
    scores = jnp.einsum("rhd,rld->rhl", query, cache_k, preferred_element_type=jnp.float32) * factor
    itself = (
        jnp.einsum("rhd,rd->rh", query, new_keys, preferred_element_type=jnp.float32) * factor
    )
    valid = (jnp.arange(length)[None, :] < lengths[:, None])[:, None, :]
    masked = jnp.where(valid, scores, -jnp.inf)
    highest = jnp.maximum(jnp.max(masked, axis=-1), itself)
    spread = jnp.exp(masked - highest[..., None])
    own_exp = jnp.exp(itself - highest)
    total = jnp.sum(spread, axis=-1) + own_exp
    weights = (spread / total[..., None]).astype(jnp.bfloat16)
    own_weight = (own_exp / total).astype(jnp.bfloat16)
    mixed = jnp.einsum("rhl,rld->rhd", weights, cache_v, preferred_element_type=jnp.float32)
    mixed = (
        mixed
        + own_weight.astype(jnp.float32)[..., None] * new_values.astype(jnp.float32)[:, None, :]
    )
    return mixed.reshape(count, -1).astype(jnp.bfloat16)


def slot_codes(route_ids, experts, capacity):
    routes = route_ids.reshape(MICRO, MB, TOP)
    onehot = (routes[..., None] == jnp.arange(experts, dtype=jnp.int32)).astype(jnp.int32)
    flat = onehot.reshape(MICRO, MB * TOP, experts)
    before = jnp.cumsum(flat, axis=1) - flat
    slots = jnp.sum(before * flat, axis=-1).reshape(MICRO, MB, TOP)
    batch = jnp.arange(MICRO, dtype=jnp.int32)[:, None, None]
    return ((routes * MICRO + batch) * capacity + slots).reshape(MICRO * MB, TOP)


def spread_over(value, axis):
    return jnp.concatenate([value] + [shift(value, axis, k) for k in range(1, SIDE)], axis=0)


def body(
    resid,
    queries,
    new_keys,
    new_values,
    cache_k,
    cache_v,
    lengths,
    out_proj,
    norm_gain,
    router,
    route_ids,
    w_gate,
    w_up,
    w_down,
):
    count, model_width = resid.shape
    experts = router.shape[1]
    capacity = 4 * MB // experts
    slots = MICRO * capacity
    share = model_width // experts
    mine = lax.axis_index(EXPERT_AXES)

    codes = slot_codes(route_ids, experts, capacity)
    places = jnp.arange(experts * slots, dtype=jnp.int32)[:, None]
    dispatch = ((codes[None, :, 0] == places) | (codes[None, :, 1] == places)).astype(jnp.bfloat16)

    heads_out = attend(queries, new_keys, new_values, cache_k, cache_v, lengths)
    partial_out = jnp.dot(heads_out, out_proj, preferred_element_type=jnp.float32).astype(
        jnp.bfloat16
    )
    partial_out = partial_out.reshape(count, experts, share).transpose(1, 0, 2)
    sums = lax.all_to_all(partial_out, EXPERT_AXES, 0, 0, tiled=True)
    own_resid = lax.dynamic_slice_in_dim(resid, mine * share, share, 1)
    state = own_resid.astype(jnp.float32) + jnp.sum(sums.astype(jnp.float32), axis=0)

    sent = jnp.dot(dispatch, state.astype(jnp.bfloat16), preferred_element_type=jnp.float32)
    sent = sent.astype(jnp.bfloat16).reshape(experts, slots, share)
    rows = lax.all_to_all(sent, EXPERT_AXES, 0, 0, tiled=True).astype(jnp.float32)
    mean_square = jnp.sum(rows * rows, axis=(0, 2)) / model_width
    gain = norm_gain.astype(jnp.float32).reshape(experts, 1, share)
    normed = (rows * lax.rsqrt(mean_square + epsilon)[None, :, None] * gain).astype(jnp.bfloat16)
    normed = normed.transpose(1, 0, 2).reshape(slots, model_width)

    logits = jnp.dot(normed, router, preferred_element_type=jnp.float32)
    own_dispatch = lax.dynamic_slice_in_dim(dispatch, mine * slots, slots, 0)
    expert_ids = jnp.arange(experts, dtype=jnp.int32)
    match = jnp.sum((route_ids[:, :, None] == expert_ids).astype(jnp.bfloat16), axis=1)
    both = jnp.dot(own_dispatch, match, preferred_element_type=jnp.float32)
    own_mask = (expert_ids == mine)[None, :]
    own_logit = jnp.sum(jnp.where(own_mask, logits, 0.0), axis=1)
    other_logit = jnp.sum(jnp.where(own_mask, 0.0, logits * both), axis=1)
    gates = (1.0 / (1.0 + jnp.exp(other_logit - own_logit))).astype(jnp.bfloat16)

    gate_weight = w_gate[0]
    up_weight = w_up[0]
    down_weight = w_down[0]

    def expert(piece):
        gate = jnp.dot(piece, gate_weight, preferred_element_type=jnp.float32)
        upper = jnp.dot(piece, up_weight, preferred_element_type=jnp.float32)
        expanded = (jax.nn.silu(gate) * upper).astype(jnp.bfloat16)
        return jnp.dot(expanded, down_weight, preferred_element_type=jnp.float32).astype(
            jnp.bfloat16
        )

    def add(one, two):
        return (one.astype(jnp.float32) + two.astype(jnp.float32)).astype(jnp.bfloat16)

    first = [spread_over(normed[:capacity], "z")]
    second = [spread_over(normed[capacity:], "y")]
    for _ in range(SIDE - 1):
        first.append(ring(first[-1], "y"))
        second.append(ring(second[-1], "z"))
    parts = []
    for one, two in zip(first, second):
        part = expert(jnp.concatenate([one, two], axis=0))
        parts.append((part[: one.shape[0]], part[one.shape[0] :]))
    one, two = parts[1]
    for step in (2, 3, 0):
        one = add(ring(one, "y"), parts[step][0])
        two = add(ring(two, "z"), parts[step][1])

    def collect(value, axis):
        pieces = value.reshape(SIDE, capacity, model_width)
        total = pieces[0].astype(jnp.float32)
        for k in range(1, SIDE):
            total = total + shift(pieces[k], axis, -k).astype(jnp.float32)
        return total

    expert_out = jnp.concatenate([collect(one, "z"), collect(two, "y")], axis=0)
    weighted = (expert_out * gates.astype(jnp.float32)[:, None]).astype(jnp.bfloat16)
    weighted = weighted.reshape(slots, experts, share).transpose(1, 0, 2)
    back = lax.all_to_all(weighted, EXPERT_AXES, 0, 0, tiled=True)
    moe = lax.dot_general(
        dispatch,
        back.reshape(experts * slots, share),
        (((0,), (0,)), ((), ())),
        preferred_element_type=jnp.float32,
    )
    return (state + moe).astype(jnp.bfloat16)


def solution(mesh):
    fine = Mesh(mesh.devices.reshape(SIDE, SIDE, SIDE, 2), ("y", "z", "x", "c"))
    attn = ("y", "z")
    placed = (
        P(attn, None),
        P(attn, EXPERT_AXES),
        P(attn, EXPERT_AXES),
        P(attn, EXPERT_AXES),
        P(attn, None, EXPERT_AXES),
        P(attn, None, EXPERT_AXES),
        P(attn),
        P(EXPERT_AXES, None),
        P(),
        P(),
        P(attn, None),
        P(EXPERT_AXES, None, attn),
        P(EXPERT_AXES, None, attn),
        P(EXPERT_AXES, attn, None),
    )
    return jax.shard_map(
        body, mesh=fine, in_specs=placed, out_specs=P(attn, EXPERT_AXES), check_vma=False
    )
```

```python
import math

import jax
import jax.numpy as jnp
from jax import lax
from jax.experimental import pallas as pl
from jax.experimental.pallas import tpu as pltpu
from jax.sharding import Mesh
from jax.sharding import PartitionSpec as P

HD = 128
TOP = 2
MICRO = 2
MB = 32
SIDE = 4
EXPERT_AXES = ("x", "c")
DEEP = 8
WIDE = 6
AHEAD = 4

epsilon = 1e-05


def shift(value, axis, step):
    return lax.ppermute(value, axis, [(i, (i + step) % SIDE) for i in range(SIDE)])


def ring(value, axis):
    perm = []
    for i in range(SIDE):
        perm.append((2 * i, 2 * ((i + 1) % SIDE)))
        perm.append((2 * i + 1, 2 * ((i - 1) % SIDE) + 1))
    return lax.ppermute(value, (axis, "c"), perm)


def swap(value, axis, turn):
    perm = []
    for i in range(SIDE):
        for core in range(2):
            partner = i ^ 1 if core == turn else SIDE - 1 - i
            perm.append((2 * i + core, 2 * partner + core))
    return lax.ppermute(value, (axis, "c"), perm)


def gather_over(value, axis):
    half = jnp.concatenate([value, swap(value, axis, 0)], axis=0)
    return jnp.concatenate([half, swap(half, axis, 1)], axis=0)


def reduce_over(value, axis):
    rows = value.shape[0] // 2
    half = add(value[:rows], swap(value[rows:], axis, 1))
    rows = rows // 2
    return half[:rows].astype(jnp.float32) + swap(half[rows:], axis, 0).astype(jnp.float32)


def add(one, two):
    return (one.astype(jnp.float32) + two.astype(jnp.float32)).astype(jnp.bfloat16)


def expert_kernel(
    first, second, w_gate, w_up, w_down, first_out, second_out, rows, gate_w, up_w, down_w, gate, upper, out, sems, out_sems
):
    count, width = first.shape
    hidden = w_gate.shape[2]
    deep = width // DEEP
    wide = width // WIDE
    copies = [
        (pltpu.make_async_copy(first, rows.at[pl.ds(0, count)], sems.at[0]),),
        (pltpu.make_async_copy(second, rows.at[pl.ds(count, count)], sems.at[1]),),
    ]
    for k in range(DEEP):
        part = pl.ds(k * deep, deep)
        copies.append(
            (
                pltpu.make_async_copy(w_gate.at[0, part], gate_w.at[part], sems.at[2 + 2 * k]),
                pltpu.make_async_copy(w_up.at[0, part], up_w.at[part], sems.at[3 + 2 * k]),
            )
        )
    for n in range(WIDE):
        part = pl.ds(n * wide, wide)
        copies.append(
            (pltpu.make_async_copy(w_down.at[0, :, part], down_w.at[:, part], sems.at[2 + 2 * DEEP + n]),)
        )

    def start(index):
        if index < len(copies):
            for copy in copies[index]:
                copy.start()

    def wait(index):
        for copy in copies[index]:
            copy.wait()

    for index in range(2 + AHEAD):
        start(index)
    wait(0)
    wait(1)
    for k in range(DEEP):
        wait(2 + k)
        start(2 + k + AHEAD)
        part = pl.ds(k * deep, deep)
        more_gate = jnp.dot(rows[:, part], gate_w[part, :], preferred_element_type=jnp.float32)
        more_up = jnp.dot(rows[:, part], up_w[part, :], preferred_element_type=jnp.float32)
        if k == 0:
            gate[...] = more_gate
            upper[...] = more_up
        else:
            gate[...] += more_gate
            upper[...] += more_up
    value = gate[...]
    expanded = (value / (1.0 + jnp.exp(-value)) * upper[...]).astype(jnp.bfloat16)
    writes = []
    for n in range(WIDE):
        wait(2 + DEEP + n)
        start(2 + DEEP + n + AHEAD)
        part = pl.ds(n * wide, wide)
        out[:, part] = jnp.dot(
            expanded, down_w[:, part], preferred_element_type=jnp.float32
        ).astype(jnp.bfloat16)
        for side, target in enumerate((first_out, second_out)):
            write = pltpu.make_async_copy(
                out.at[pl.ds(side * count, count), part], target.at[:, part], out_sems.at[2 * n + side]
            )
            write.start()
            writes.append(write)
    for write in writes:
        write.wait()


def expert(first, second, w_gate, w_up, w_down):
    count, width = first.shape
    hidden = w_gate.shape[2]
    shape = jax.ShapeDtypeStruct((count, width), jnp.bfloat16)
    anywhere = pl.BlockSpec(memory_space=pl.ANY)
    return pl.pallas_call(
        expert_kernel,
        out_shape=(shape, shape),
        in_specs=[anywhere] * 5,
        out_specs=(anywhere, anywhere),
        scratch_shapes=[
            pltpu.VMEM((2 * count, width), jnp.bfloat16),
            pltpu.VMEM((width, hidden), jnp.bfloat16),
            pltpu.VMEM((width, hidden), jnp.bfloat16),
            pltpu.VMEM((hidden, width), jnp.bfloat16),
            pltpu.VMEM((2 * count, hidden), jnp.float32),
            pltpu.VMEM((2 * count, hidden), jnp.float32),
            pltpu.VMEM((2 * count, width), jnp.bfloat16),
            pltpu.SemaphoreType.DMA((2 + 2 * DEEP + WIDE,)),
            pltpu.SemaphoreType.DMA((2 * WIDE,)),
        ],
        compiler_params=pltpu.CompilerParams(vmem_limit_bytes=40 * 1024 * 1024),
        cost_estimate=pl.CostEstimate(
            flops=12 * count * width * hidden, bytes_accessed=6 * width * hidden, transcendentals=0
        ),
        name="expert_rows",
    )(first, second, w_gate, w_up, w_down)


def attend(queries, new_keys, new_values, cache_k, cache_v, lengths):
    count = queries.shape[0]
    length = cache_k.shape[1]
    group = queries.shape[1] // HD
    query = queries.reshape(count, group, HD)
    factor = 1.0 / math.sqrt(HD)
    scores = jnp.einsum("rhd,rld->rhl", query, cache_k, preferred_element_type=jnp.float32) * factor
    itself = (
        jnp.einsum("rhd,rd->rh", query, new_keys, preferred_element_type=jnp.float32) * factor
    )
    valid = (jnp.arange(length)[None, :] < lengths[:, None])[:, None, :]
    masked = jnp.where(valid, scores, -jnp.inf)
    highest = jnp.maximum(jnp.max(masked, axis=-1), itself)
    spread = jnp.exp(masked - highest[..., None])
    own_exp = jnp.exp(itself - highest)
    total = jnp.sum(spread, axis=-1) + own_exp
    weights = (spread / total[..., None]).astype(jnp.bfloat16)
    own_weight = (own_exp / total).astype(jnp.bfloat16)
    mixed = jnp.einsum("rhl,rld->rhd", weights, cache_v, preferred_element_type=jnp.float32)
    mixed = (
        mixed
        + own_weight.astype(jnp.float32)[..., None] * new_values.astype(jnp.float32)[:, None, :]
    )
    return mixed.reshape(count, -1).astype(jnp.bfloat16)


def slot_codes(routes, experts, capacity):
    onehot = (routes[..., None] == jnp.arange(experts, dtype=jnp.int32)).astype(jnp.int32)
    flat = onehot.reshape(MB * TOP, experts)
    before = jnp.cumsum(flat, axis=0) - flat
    return routes * capacity + jnp.sum(before * flat, axis=-1).reshape(MB, TOP)


def body(
    resid,
    queries,
    new_keys,
    new_values,
    cache_k,
    cache_v,
    lengths,
    out_proj,
    norm_gain,
    router,
    route_ids,
    w_gate,
    w_up,
    w_down,
):
    model_width = resid.shape[1]
    experts = router.shape[1]
    capacity = 4 * MB // experts
    share = model_width // experts
    mine = lax.axis_index(EXPERT_AXES)
    places = jnp.arange(experts * capacity, dtype=jnp.int32)[:, None]
    expert_ids = jnp.arange(experts, dtype=jnp.int32)
    own_mask = (expert_ids == mine)[None, :]
    gain = norm_gain.astype(jnp.float32).reshape(experts, 1, share)
    own_resid = lax.dynamic_slice_in_dim(resid, mine * share, share, 1)

    def prepare(batch):
        def part(array):
            return lax.slice_in_dim(array, batch * MB, (batch + 1) * MB, axis=0)

        routes = part(route_ids)
        codes = slot_codes(routes, experts, capacity)
        dispatch = ((codes[None, :, 0] == places) | (codes[None, :, 1] == places)).astype(
            jnp.bfloat16
        )
        heads_out = attend(
            part(queries),
            part(new_keys),
            part(new_values),
            part(cache_k),
            part(cache_v),
            part(lengths),
        )
        partial_out = jnp.dot(heads_out, out_proj, preferred_element_type=jnp.float32).astype(
            jnp.bfloat16
        )
        partial_out = partial_out.reshape(MB, experts, share).transpose(1, 0, 2)
        sums = lax.all_to_all(partial_out, EXPERT_AXES, 0, 0, tiled=True)
        state = part(own_resid).astype(jnp.float32) + jnp.sum(sums.astype(jnp.float32), axis=0)

        sent = jnp.dot(dispatch, state.astype(jnp.bfloat16), preferred_element_type=jnp.float32)
        sent = sent.astype(jnp.bfloat16).reshape(experts, capacity, share)
        rows = lax.all_to_all(sent, EXPERT_AXES, 0, 0, tiled=True).astype(jnp.float32)
        mean_square = jnp.sum(rows * rows, axis=(0, 2)) / model_width
        normed = (rows * lax.rsqrt(mean_square + epsilon)[None, :, None] * gain).astype(
            jnp.bfloat16
        )
        normed = normed.transpose(1, 0, 2).reshape(capacity, model_width)

        logits = jnp.dot(normed, router, preferred_element_type=jnp.float32)
        own_dispatch = lax.dynamic_slice_in_dim(dispatch, mine * capacity, capacity, 0)
        match = jnp.sum((routes[:, :, None] == expert_ids).astype(jnp.bfloat16), axis=1)
        both = jnp.dot(own_dispatch, match, preferred_element_type=jnp.float32)
        own_logit = jnp.sum(jnp.where(own_mask, logits, 0.0), axis=1)
        other_logit = jnp.sum(jnp.where(own_mask, 0.0, logits * both), axis=1)
        gates = (1.0 / (1.0 + jnp.exp(other_logit - own_logit))).astype(jnp.bfloat16)
        return state, dispatch, normed, gates

    def finish(state, dispatch, gates, expert_out):
        weighted = (expert_out * gates.astype(jnp.float32)[:, None]).astype(jnp.bfloat16)
        weighted = weighted.reshape(capacity, experts, share).transpose(1, 0, 2)
        back = lax.all_to_all(weighted, EXPERT_AXES, 0, 0, tiled=True)
        moe = lax.dot_general(
            dispatch,
            back.reshape(experts * capacity, share),
            (((0,), (0,)), ((), ())),
            preferred_element_type=jnp.float32,
        )
        return (state + moe).astype(jnp.bfloat16)

    ready = [prepare(batch) for batch in range(MICRO)]
    first = [gather_over(ready[0][2], "z")]
    second = [gather_over(ready[1][2], "y")]
    for _ in range(SIDE - 1):
        first.append(ring(first[-1], "y"))
        second.append(ring(second[-1], "z"))
    parts = [expert(one, two, w_gate, w_up, w_down) for one, two in zip(first, second)]
    one, two = parts[1]
    for step in (2, 3, 0):
        one = add(ring(one, "y"), parts[step][0])
        two = add(ring(two, "z"), parts[step][1])
    outs = []
    for (state, dispatch, _, gates), total, axis in zip(ready, (one, two), ("z", "y")):
        outs.append(finish(state, dispatch, gates, reduce_over(total, axis)))
    return jnp.concatenate(outs, axis=0)


def solution(mesh):
    fine = Mesh(mesh.devices.reshape(SIDE, SIDE, SIDE, 2), ("y", "z", "x", "c"))
    attn = ("y", "z")
    placed = (
        P(attn, None),
        P(attn, EXPERT_AXES),
        P(attn, EXPERT_AXES),
        P(attn, EXPERT_AXES),
        P(attn, None, EXPERT_AXES),
        P(attn, None, EXPERT_AXES),
        P(attn),
        P(EXPERT_AXES, None),
        P(),
        P(),
        P(attn, None),
        P(EXPERT_AXES, None, attn),
        P(EXPERT_AXES, None, attn),
        P(EXPERT_AXES, attn, None),
    )
    return jax.shard_map(
        body, mesh=fine, in_specs=placed, out_specs=P(attn, EXPERT_AXES), check_vma=False
    )
```

```python
import math

import jax
import jax.numpy as jnp
from jax import lax
from jax.experimental import pallas as pl
from jax.experimental.pallas import tpu as pltpu
from jax.sharding import Mesh
from jax.sharding import PartitionSpec as P

HD = 128
TOP = 2
MICRO = 2
MB = 32
SIDE = 4
EXPERT_AXES = ("x", "c")
DEEP = 8
WIDE = 6
BLOCK = 32
EXPERT_VMEM = 8 * 1024 * 1024
VMEM = 60 * 1024 * 1024

epsilon = 1e-05


def shift(value, axis, step):
    return lax.ppermute(value, axis, [(i, (i + step) % SIDE) for i in range(SIDE)])


def ring(value, axis, turn):
    perm = []
    for i in range(SIDE):
        for core in range(2):
            to = (i + (1 if core == turn else -1)) % SIDE
            perm.append((2 * i + core, 2 * to + core))
    return lax.ppermute(value, (axis, "c"), perm)


def swap(value, axis, turn):
    perm = []
    for i in range(SIDE):
        for core in range(2):
            partner = i ^ 1 if core == turn else SIDE - 1 - i
            perm.append((2 * i + core, 2 * partner + core))
    return lax.ppermute(value, (axis, "c"), perm)


def gather_over(value, axis):
    half = jnp.concatenate([value, swap(value, axis, 0)], axis=0)
    return jnp.concatenate([half, swap(half, axis, 1)], axis=0)


def reduce_over(value, axis):
    rows = value.shape[0] // 2
    half = add(value[:rows], swap(value[rows:], axis, 1))
    rows = rows // 2
    return half[:rows].astype(jnp.float32) + swap(half[rows:], axis, 0).astype(jnp.float32)


def add(one, two):
    return (one.astype(jnp.float32) + two.astype(jnp.float32)).astype(jnp.bfloat16)


def expert_steps(first, second, weights, outs, scratch, arrive):
    w_gate, w_up, w_down = weights
    rows, gate, upper, out, in_sems, out_sems = scratch
    count, width = first.shape
    deep = width // DEEP
    wide = width // WIDE
    halves = [pl.ds(side * count, count) for side in range(2)]
    for side, source in enumerate((first, second)):
        pltpu.make_async_copy(source, rows.at[halves[side]], in_sems.at[side]).wait()
    for k in range(DEEP):
        arrive(k)
        part = pl.ds(k * deep, deep)
        more_gate = jnp.dot(rows[:, part], w_gate[part, :], preferred_element_type=jnp.float32)
        more_up = jnp.dot(rows[:, part], w_up[part, :], preferred_element_type=jnp.float32)
        if k == 0:
            gate[...] = more_gate
            upper[...] = more_up
        else:
            gate[...] += more_gate
            upper[...] += more_up
    value = gate[...]
    expanded = (value / (1.0 + jnp.exp(-value)) * upper[...]).astype(jnp.bfloat16)
    writes = []
    for n in range(WIDE):
        arrive(DEEP + n)
        part = pl.ds(n * wide, wide)
        out[:, part] = jnp.dot(
            expanded, w_down[:, part], preferred_element_type=jnp.float32
        ).astype(jnp.bfloat16)
        for side, target in enumerate(outs):
            write = pltpu.make_async_copy(
                out.at[halves[side], part], target.at[:, part], out_sems.at[2 * n + side]
            )
            write.start()
            writes.append(write)
    for write in writes:
        write.wait()


def start_rows(first, second, rows, in_sems):
    count = first.shape[0]
    for side, source in enumerate((first, second)):
        pltpu.make_async_copy(
            source, rows.at[pl.ds(side * count, count)], in_sems.at[side]
        ).start()


def expert_kernel(first, second, w_gate, w_up, w_down, first_out, second_out, *scratch):
    start_rows(first, second, scratch[0], scratch[4])
    expert_steps(
        first, second, (w_gate, w_up, w_down), (first_out, second_out), scratch, lambda k: None
    )


def first_expert_kernel(
    first, second, w_gate, w_up, w_down, first_out, second_out, kept_gate, kept_up, kept_down, *scratch
):
    deep = w_gate.shape[1] // DEEP
    wide = w_down.shape[2] // WIDE
    sems = scratch[6]
    groups = []
    for k in range(DEEP):
        part = pl.ds(k * deep, deep)
        groups.append(
            (
                pltpu.make_async_copy(w_gate.at[0, part], kept_gate.at[part], sems.at[2 * k]),
                pltpu.make_async_copy(w_up.at[0, part], kept_up.at[part], sems.at[2 * k + 1]),
            )
        )
    for n in range(WIDE):
        part = pl.ds(n * wide, wide)
        groups.append(
            (
                pltpu.make_async_copy(
                    w_down.at[0, :, part], kept_down.at[:, part], sems.at[2 * DEEP + n]
                ),
            )
        )
    start_rows(first, second, scratch[0], scratch[4])
    for group in groups:
        for copy in group:
            copy.start()

    def arrive(k):
        for copy in groups[k]:
            copy.wait()

    expert_steps(
        first, second, (kept_gate, kept_up, kept_down), (first_out, second_out), scratch[:6], arrive
    )


def expert_call(kernel, first, second, weights, hidden, kept):
    count, width = first.shape
    anywhere = pl.BlockSpec(memory_space=pl.ANY)
    near = pl.BlockSpec(memory_space=pltpu.VMEM)
    outs = [jax.ShapeDtypeStruct((count, width), jnp.bfloat16)] * 2
    scratch = [
        pltpu.VMEM((2 * count, width), jnp.bfloat16),
        pltpu.VMEM((2 * count, hidden), jnp.float32),
        pltpu.VMEM((2 * count, hidden), jnp.float32),
        pltpu.VMEM((2 * count, width), jnp.bfloat16),
        pltpu.SemaphoreType.DMA((2,)),
        pltpu.SemaphoreType.DMA((2 * WIDE,)),
    ]
    if kept:
        weights = [pltpu.with_memory_space_constraint(w, pltpu.VMEM) for w in weights]
    else:
        weights = [pltpu.with_memory_space_constraint(w, pltpu.HBM) for w in weights]
        outs += [pltpu.VMEM(w.shape[1:], w.dtype) for w in weights]
        scratch.append(pltpu.SemaphoreType.DMA((2 * DEEP + WIDE,)))
    return pl.pallas_call(
        kernel,
        out_shape=tuple(outs),
        in_specs=[anywhere] * 2 + [near if kept else anywhere] * 3,
        out_specs=(anywhere,) * 2 + (near,) * (len(outs) - 2),
        scratch_shapes=scratch,
        compiler_params=pltpu.CompilerParams(vmem_limit_bytes=EXPERT_VMEM),
        cost_estimate=pl.CostEstimate(flops=1000000, bytes_accessed=100000, transcendentals=0),
        name="expert_rows" if kept else "expert_rows_first",
    )(first, second, *weights)


def hold_kernel(*refs):
    pass


def hold(values, after):
    anywhere = pl.BlockSpec(memory_space=pl.ANY)
    return pl.pallas_call(
        hold_kernel,
        out_shape=tuple(jax.ShapeDtypeStruct(v.shape, v.dtype) for v in values),
        in_specs=[anywhere] * (len(values) + len(after)),
        out_specs=(anywhere,) * len(values),
        input_output_aliases={i: i for i in range(len(values))},
        compiler_params=pltpu.CompilerParams(vmem_limit_bytes=1024 * 1024),
        cost_estimate=pl.CostEstimate(flops=1000, bytes_accessed=1000, transcendentals=0),
        name="hold_rows",
    )(*values, *after)


def attend_kernel(
    where, queries, new_keys, new_values, cache_k, cache_v, lengths, out_proj, mine, theirs, heads, weights, sem
):
    step = pl.program_id(0)
    block = queries.shape[0]
    length = cache_k.shape[1]
    group = queries.shape[1] // HD
    half = 8
    copy = pltpu.make_async_copy(out_proj, weights, sem)

    @pl.when(step == 0)
    def _():
        copy.start()

    factor = 1.0 / math.sqrt(HD)
    column = lax.broadcasted_iota(jnp.int32, (group * half, half * length), 1)
    line = lax.broadcasted_iota(jnp.int32, (group * half, half * length), 0)
    same_row = column // length == line % half
    position = column % length
    turn = lax.broadcasted_iota(jnp.int32, (group * half, 1), 0) % half
    all_queries = queries[...].astype(jnp.float32)
    all_keys = new_keys[...].astype(jnp.float32)
    all_values = new_values[...].astype(jnp.float32)
    outs = []
    for part in range(block // half):
        rows = slice(part * half, (part + 1) * half)
        query = jnp.concatenate(
            [all_queries[rows, h * HD : (h + 1) * HD] for h in range(group)], axis=0
        )
        fresh_key = jnp.concatenate([all_keys[rows]] * group, axis=0)
        fresh_value = jnp.concatenate([all_values[rows]] * group, axis=0)
        used = jnp.zeros((group * half, 1), jnp.int32)
        for r in range(half):
            used = jnp.where(turn == r, lengths[step * block + part * half + r], used)
        keys = cache_k[rows].reshape(half * length, HD)
        values = cache_v[rows].reshape(half * length, HD)
        scores = (
            lax.dot_general(
                query.astype(jnp.bfloat16),
                keys,
                (((1,), (1,)), ((), ())),
                preferred_element_type=jnp.float32,
            )
            * factor
        )
        itself = jnp.sum(query * fresh_key, axis=1, keepdims=True) * factor
        masked = jnp.where(same_row & (position < used), scores, -jnp.inf)
        highest = jnp.maximum(jnp.max(masked, axis=1, keepdims=True), itself)
        spread = jnp.exp(masked - highest)
        own_exp = jnp.exp(itself - highest)
        inverse = 1.0 / (jnp.sum(spread, axis=1, keepdims=True) + own_exp)
        probs = (spread * inverse).astype(jnp.bfloat16)
        own_prob = (own_exp * inverse).astype(jnp.bfloat16).astype(jnp.float32)
        mixed = jnp.dot(probs, values, preferred_element_type=jnp.float32) + own_prob * fresh_value
        outs.append(
            jnp.concatenate([mixed[h * half : (h + 1) * half] for h in range(group)], axis=1)
        )
    heads[pl.ds(step * block, block), :] = jnp.concatenate(outs, axis=0).astype(jnp.bfloat16)

    @pl.when(step == pl.num_programs(0) - 1)
    def _():
        copy.wait()
        share = mine.shape[2]
        left = heads[...]
        for k in range(SIDE):
            chip = lax.rem(where[0] + k, SIDE)
            for core, target in ((where[1], mine), (1 - where[1], theirs)):
                part = pl.ds(pl.multiple_of((chip * 2 + core) * share, share), share)
                target[k] = jnp.dot(
                    left, weights[:, part], preferred_element_type=jnp.float32
                ).astype(jnp.bfloat16)


def attend(where, queries, new_keys, new_values, cache_k, cache_v, lengths, out_proj):
    count, width = queries.shape
    length = cache_k.shape[1]
    share = out_proj.shape[1] // (2 * SIDE)
    shape = jax.ShapeDtypeStruct((SIDE, count, share), jnp.bfloat16)
    whole = pl.BlockSpec((SIDE, count, share), lambda i: (0, 0, 0))
    return pl.pallas_call(
        attend_kernel,
        grid=(count // BLOCK,),
        out_shape=(shape, shape),
        in_specs=[
            pl.BlockSpec(memory_space=pltpu.SMEM),
            pl.BlockSpec((BLOCK, width), lambda i: (i, 0)),
            pl.BlockSpec((BLOCK, HD), lambda i: (i, 0)),
            pl.BlockSpec((BLOCK, HD), lambda i: (i, 0)),
            pl.BlockSpec((BLOCK, length, HD), lambda i: (i, 0, 0)),
            pl.BlockSpec((BLOCK, length, HD), lambda i: (i, 0, 0)),
            pl.BlockSpec(memory_space=pltpu.SMEM),
            pl.BlockSpec(memory_space=pl.ANY),
        ],
        out_specs=(whole, whole),
        scratch_shapes=[
            pltpu.VMEM((count, width), jnp.bfloat16),
            pltpu.VMEM(out_proj.shape, jnp.bfloat16),
            pltpu.SemaphoreType.DMA(()),
        ],
        compiler_params=pltpu.CompilerParams(vmem_limit_bytes=VMEM),
        cost_estimate=pl.CostEstimate(
            flops=2 * count * width * out_proj.shape[1],
            bytes_accessed=4 * count * length * HD,
            transcendentals=0,
        ),
        name="attend_rows",
    )(where, queries, new_keys, new_values, cache_k, cache_v, lengths, out_proj)


def slot_codes(route_ids, experts, capacity):
    routes = route_ids.reshape(MICRO, MB, TOP)
    onehot = (routes[..., None] == jnp.arange(experts, dtype=jnp.int32)).astype(jnp.int32)
    flat = onehot.reshape(MICRO, MB * TOP, experts)
    before = jnp.cumsum(flat, axis=1) - flat
    slots = jnp.sum(before * flat, axis=-1).reshape(MICRO, MB, TOP)
    batch = jnp.arange(MICRO, dtype=jnp.int32)[:, None, None]
    return ((routes * MICRO + batch) * capacity + slots).reshape(MICRO * MB, TOP)


def body(
    resid,
    queries,
    new_keys,
    new_values,
    cache_k,
    cache_v,
    lengths,
    out_proj,
    norm_gain,
    router,
    route_ids,
    w_gate,
    w_up,
    w_down,
):
    count, model_width = resid.shape
    experts = router.shape[1]
    capacity = 4 * MB // experts
    slots = MICRO * capacity
    share = model_width // experts
    mine = lax.axis_index(EXPERT_AXES)
    where = jnp.stack([lax.axis_index("x"), lax.axis_index("c")]).astype(jnp.int32)

    own, others = attend(
        where, queries, new_keys, new_values, cache_k, cache_v, lengths, out_proj
    )
    arrived = lax.ppermute(others, "c", [(0, 1), (1, 0)])
    sums = [add(own[k], arrived[k]) for k in range(SIDE)]
    sums = [sums[0]] + [shift(sums[k], "x", k) for k in range(1, SIDE)]

    route_ids, _ = lax.optimization_barrier((route_ids, own))
    codes = slot_codes(route_ids, experts, capacity)
    places = jnp.arange(experts * slots, dtype=jnp.int32)[:, None]
    dispatch = ((codes[None, :, 0] == places) | (codes[None, :, 1] == places)).astype(jnp.bfloat16)
    slot = jnp.arange(slots, dtype=jnp.int32)[:, None]
    hits = [(c // slots == mine)[None] & (c % slots == slot) for c in (codes[:, 0], codes[:, 1])]
    own_dispatch = (hits[0] | hits[1]).astype(jnp.bfloat16)
    expert_ids = jnp.arange(experts, dtype=jnp.int32)
    match = jnp.sum((route_ids[:, :, None] == expert_ids).astype(jnp.bfloat16), axis=1)
    both = jnp.dot(own_dispatch, match, preferred_element_type=jnp.float32)
    own_mask = (expert_ids == mine)[None, :]

    state = lax.dynamic_slice_in_dim(resid, mine * share, share, 1).astype(jnp.float32)
    for one in sums:
        state = state + one.astype(jnp.float32)
    sent = jnp.dot(dispatch, state.astype(jnp.bfloat16), preferred_element_type=jnp.float32)
    sent = sent.astype(jnp.bfloat16).reshape(experts, slots, share)
    rows = lax.all_to_all(sent, EXPERT_AXES, 0, 0, tiled=True).astype(jnp.float32)
    mean_square = jnp.sum(rows * rows, axis=(0, 2)) / model_width
    gain = norm_gain.astype(jnp.float32).reshape(experts, 1, share)
    normed = (rows * lax.rsqrt(mean_square + epsilon)[None, :, None] * gain).astype(jnp.bfloat16)
    normed = normed.transpose(1, 0, 2).reshape(slots, model_width)

    pieces = [(gather_over(normed[:capacity], "z"), gather_over(normed[capacity:], "y"))]
    (one, two), normed = lax.optimization_barrier((pieces[0], normed))

    logits = jnp.dot(normed, router, preferred_element_type=jnp.float32)
    own_logit = jnp.sum(jnp.where(own_mask, logits, 0.0), axis=1)
    other_logit = jnp.sum(jnp.where(own_mask, 0.0, logits * both), axis=1)
    gates = (1.0 / (1.0 + jnp.exp(other_logit - own_logit))).astype(jnp.bfloat16)

    def step(pair, turn):
        return ring(pair[0], "y", turn), ring(pair[1], "z", turn)

    hidden = w_gate.shape[2]

    def work(pair):
        return expert_call(expert_kernel, *pair, kept, hidden, True)

    def join(left, right):
        return add(left[0], right[0]), add(left[1], right[1])

    piece = (one, two)
    behind = step(piece, 0)
    *own_part, kept_gate, kept_up, kept_down = expert_call(
        first_expert_kernel, *piece, (w_gate, w_up, w_down), hidden, False
    )
    kept = (kept_gate, kept_up, kept_down)
    behind, own_part = lax.optimization_barrier((behind, own_part))
    far = step(behind, 0)
    behind_part = work(behind)
    ahead = step(hold(piece, far), 1)
    far_part = work(far)
    far_sum = step(far_part, 1)
    ahead, far_part = lax.optimization_barrier((ahead, far_part))
    ahead_part = work(ahead)
    from_behind = step(ahead_part, 0)
    far_sum, ahead_part = lax.optimization_barrier((far_sum, ahead_part))
    from_ahead = step(join(far_sum, behind_part), 1)

    def total(side):
        value = own_part[side].astype(jnp.float32) + from_behind[side].astype(jnp.float32)
        return (value + from_ahead[side].astype(jnp.float32)).astype(jnp.bfloat16)

    one, two = total(0), total(1)

    expert_out = jnp.concatenate([reduce_over(one, "z"), reduce_over(two, "y")], axis=0)
    weighted = (expert_out * gates.astype(jnp.float32)[:, None]).astype(jnp.bfloat16)
    weighted = weighted.reshape(slots, experts, share).transpose(1, 0, 2)
    back = lax.all_to_all(weighted, EXPERT_AXES, 0, 0, tiled=True)
    moe = lax.dot_general(
        dispatch,
        back.reshape(experts * slots, share),
        (((0,), (0,)), ((), ())),
        preferred_element_type=jnp.float32,
    )
    return (state + moe).astype(jnp.bfloat16)


def solution(mesh):
    fine = Mesh(mesh.devices.reshape(SIDE, SIDE, SIDE, 2), ("y", "z", "x", "c"))
    attn = ("y", "z")
    placed = (
        P(attn, None),
        P(attn, EXPERT_AXES),
        P(attn, EXPERT_AXES),
        P(attn, EXPERT_AXES),
        P(attn, None, EXPERT_AXES),
        P(attn, None, EXPERT_AXES),
        P(attn),
        P(EXPERT_AXES, None),
        P(),
        P(),
        P(attn, None),
        P(EXPERT_AXES, None, attn),
        P(EXPERT_AXES, None, attn),
        P(EXPERT_AXES, attn, None),
    )
    return jax.shard_map(
        body, mesh=fine, in_specs=placed, out_specs=P(attn, EXPERT_AXES), check_vma=False
    )
```

```python
import functools
import math

import jax
import jax.numpy as jnp
from jax import lax
from jax.experimental import pallas as pl
from jax.experimental.pallas import tpu as pltpu
from jax.sharding import Mesh
from jax.sharding import PartitionSpec as P

HD = 128
TOP = 2
MICRO = 2
MB = 32
SIDE = 4
EXPERT_AXES = ("x", "c")
DEEP = 8
WIDE = 6
BLOCK = 32
EXPERT_VMEM = 8 * 1024 * 1024
VMEM = 60 * 1024 * 1024

epsilon = 1e-05


def shift(value, axis, step):
    return lax.ppermute(value, axis, [(i, (i + step) % SIDE) for i in range(SIDE)])


def ring(value, axis, turn):
    perm = []
    for i in range(SIDE):
        for core in range(2):
            to = (i + (1 if core == turn else -1)) % SIDE
            perm.append((2 * i + core, 2 * to + core))
    return lax.ppermute(value, (axis, "c"), perm)


def swap(value, axis, turn):
    perm = []
    for i in range(SIDE):
        for core in range(2):
            partner = i ^ 1 if core == turn else SIDE - 1 - i
            perm.append((2 * i + core, 2 * partner + core))
    return lax.ppermute(value, (axis, "c"), perm)


def add(one, two):
    return (one.astype(jnp.float32) + two.astype(jnp.float32)).astype(jnp.bfloat16)


def expert_kernel(taken, given, kept, waits, *refs):
    sources, refs = refs[: len(taken)], refs[len(taken) :]
    weights, refs = refs[:3], refs[3 + waits :]
    targets, refs = refs[: len(given)], refs[len(given) :]
    if not kept:
        near, refs = refs[:3], refs[3:]
        weight_sems, refs = refs[-1], refs[:-1]
    rows, gate, upper, out, in_sems, out_sems = refs
    width = rows.shape[1]
    deep = width // DEEP
    wide = width // WIDE

    arrivals = []
    place = 0
    for index, (source, count) in enumerate(zip(sources, taken)):
        arrivals.append(
            pltpu.make_async_copy(source, rows.at[pl.ds(place, count)], in_sems.at[index])
        )
        place += count
    for copy in arrivals:
        copy.start()
    groups = [()] * (DEEP + WIDE)
    if not kept:
        groups = []
        for k in range(DEEP):
            part = pl.ds(k * deep, deep)
            groups.append(
                tuple(
                    pltpu.make_async_copy(
                        weights[w].at[0, part], near[w].at[part], weight_sems.at[2 * k + w]
                    )
                    for w in range(2)
                )
            )
        for n in range(WIDE):
            part = pl.ds(n * wide, wide)
            groups.append(
                (
                    pltpu.make_async_copy(
                        weights[2].at[0, :, part], near[2].at[:, part], weight_sems.at[2 * DEEP + n]
                    ),
                )
            )
        for group in groups:
            for copy in group:
                copy.start()
        weights = near
    w_gate, w_up, w_down = weights
    for copy in arrivals:
        copy.wait()

    for k in range(DEEP):
        for copy in groups[k]:
            copy.wait()
        part = pl.ds(k * deep, deep)
        more_gate = jnp.dot(rows[:, part], w_gate[part, :], preferred_element_type=jnp.float32)
        more_up = jnp.dot(rows[:, part], w_up[part, :], preferred_element_type=jnp.float32)
        if k == 0:
            gate[...] = more_gate
            upper[...] = more_up
        else:
            gate[...] += more_gate
            upper[...] += more_up
    value = gate[...]
    expanded = (value / (1.0 + jnp.exp(-value)) * upper[...]).astype(jnp.bfloat16)
    writes = []
    for n in range(WIDE):
        for copy in groups[DEEP + n]:
            copy.wait()
        part = pl.ds(n * wide, wide)
        out[:, part] = jnp.dot(
            expanded, w_down[:, part], preferred_element_type=jnp.float32
        ).astype(jnp.bfloat16)
        place = 0
        for index, (target, count) in enumerate(zip(targets, given)):
            write = pltpu.make_async_copy(
                out.at[pl.ds(place, count), part],
                target.at[:, part],
                out_sems.at[n * len(given) + index],
            )
            write.start()
            writes.append(write)
            place += count
    for write in writes:
        write.wait()


def expert_call(pieces, given, weights, kept, after=()):
    taken = tuple(p.shape[0] for p in pieces)
    total, width = sum(taken), pieces[0].shape[1]
    hidden = weights[2].shape[-2]
    anywhere = pl.BlockSpec(memory_space=pl.ANY)
    near = pl.BlockSpec(memory_space=pltpu.VMEM)
    outs = [jax.ShapeDtypeStruct((count, width), jnp.bfloat16) for count in given]
    scratch = [
        pltpu.VMEM((total, width), jnp.bfloat16),
        pltpu.VMEM((total, hidden), jnp.float32),
        pltpu.VMEM((total, hidden), jnp.float32),
        pltpu.VMEM((total, width), jnp.bfloat16),
        pltpu.SemaphoreType.DMA((len(taken),)),
        pltpu.SemaphoreType.DMA((len(given) * WIDE,)),
    ]
    if kept:
        weights = [pltpu.with_memory_space_constraint(w, pltpu.VMEM) for w in weights]
    else:
        weights = [pltpu.with_memory_space_constraint(w, pltpu.HBM) for w in weights]
        outs += [pltpu.VMEM(w.shape[1:], w.dtype) for w in weights]
        scratch.append(pltpu.SemaphoreType.DMA((2 * DEEP + WIDE,)))
    results = pl.pallas_call(
        functools.partial(expert_kernel, taken, given, kept, len(after)),
        out_shape=tuple(outs),
        in_specs=[anywhere] * len(taken)
        + [near if kept else anywhere] * 3
        + [anywhere] * len(after),
        out_specs=(anywhere,) * len(given) + (near,) * (len(outs) - len(given)),
        scratch_shapes=scratch,
        compiler_params=pltpu.CompilerParams(vmem_limit_bytes=EXPERT_VMEM),
        cost_estimate=pl.CostEstimate(flops=1000000, bytes_accessed=100000, transcendentals=0),
        name="expert_rows" if kept else "expert_rows_first",
    )(*pieces, *weights, *after)
    return results[: len(given)], results[len(given) :]


def lay_kernel(count, *refs):
    pieces, outs, sems = refs[:count], refs[-1 - count // 2 : -1], refs[-1]
    copies = []
    for index, piece in enumerate(pieces):
        rows = piece.shape[0]
        target = outs[index // 2].at[pl.ds(index % 2 * rows, rows)]
        copies.append(pltpu.make_async_copy(piece, target, sems.at[index]))
    for copy in copies:
        copy.start()
    for copy in copies:
        copy.wait()


def lay(pieces, after):
    anywhere = pl.BlockSpec(memory_space=pl.ANY)
    rows, width = pieces[0].shape
    shape = jax.ShapeDtypeStruct((2 * rows, width), pieces[0].dtype)
    return pl.pallas_call(
        functools.partial(lay_kernel, len(pieces)),
        out_shape=(shape,) * (len(pieces) // 2),
        in_specs=[anywhere] * (len(pieces) + len(after)),
        out_specs=(anywhere,) * (len(pieces) // 2),
        scratch_shapes=[pltpu.SemaphoreType.DMA((len(pieces),))],
        compiler_params=pltpu.CompilerParams(vmem_limit_bytes=1024 * 1024),
        cost_estimate=pl.CostEstimate(flops=1000, bytes_accessed=1000, transcendentals=0),
        name="lay_rows",
    )(*pieces, *after)


def attend_kernel(
    where, queries, new_keys, new_values, cache_k, cache_v, lengths, out_proj, mine, theirs, heads, weights, sem
):
    step = pl.program_id(0)
    block = queries.shape[0]
    length = cache_k.shape[1]
    group = queries.shape[1] // HD
    half = 8
    copy = pltpu.make_async_copy(out_proj, weights, sem)

    @pl.when(step == 0)
    def _():
        copy.start()

    factor = 1.0 / math.sqrt(HD)
    column = lax.broadcasted_iota(jnp.int32, (group * half, half * length), 1)
    line = lax.broadcasted_iota(jnp.int32, (group * half, half * length), 0)
    same_row = column // length == line % half
    position = column % length
    turn = lax.broadcasted_iota(jnp.int32, (group * half, 1), 0) % half
    all_queries = queries[...].astype(jnp.float32)
    all_keys = new_keys[...].astype(jnp.float32)
    all_values = new_values[...].astype(jnp.float32)
    outs = []
    for part in range(block // half):
        rows = slice(part * half, (part + 1) * half)
        query = jnp.concatenate(
            [all_queries[rows, h * HD : (h + 1) * HD] for h in range(group)], axis=0
        )
        fresh_key = jnp.concatenate([all_keys[rows]] * group, axis=0)
        fresh_value = jnp.concatenate([all_values[rows]] * group, axis=0)
        used = jnp.zeros((group * half, 1), jnp.int32)
        for r in range(half):
            used = jnp.where(turn == r, lengths[step * block + part * half + r], used)
        keys = cache_k[rows].reshape(half * length, HD)
        values = cache_v[rows].reshape(half * length, HD)
        scores = (
            lax.dot_general(
                query.astype(jnp.bfloat16),
                keys,
                (((1,), (1,)), ((), ())),
                preferred_element_type=jnp.float32,
            )
            * factor
        )
        itself = jnp.sum(query * fresh_key, axis=1, keepdims=True) * factor
        masked = jnp.where(same_row & (position < used), scores, -jnp.inf)
        highest = jnp.maximum(jnp.max(masked, axis=1, keepdims=True), itself)
        spread = jnp.exp(masked - highest)
        own_exp = jnp.exp(itself - highest)
        inverse = 1.0 / (jnp.sum(spread, axis=1, keepdims=True) + own_exp)
        probs = (spread * inverse).astype(jnp.bfloat16)
        own_prob = (own_exp * inverse).astype(jnp.bfloat16).astype(jnp.float32)
        mixed = jnp.dot(probs, values, preferred_element_type=jnp.float32) + own_prob * fresh_value
        outs.append(
            jnp.concatenate([mixed[h * half : (h + 1) * half] for h in range(group)], axis=1)
        )
    heads[pl.ds(step * block, block), :] = jnp.concatenate(outs, axis=0).astype(jnp.bfloat16)

    @pl.when(step == pl.num_programs(0) - 1)
    def _():
        copy.wait()
        share = mine.shape[2]
        left = heads[...]
        for k in range(SIDE):
            chip = lax.rem(where[0] + k, SIDE)
            for core, target in ((where[1], mine), (1 - where[1], theirs)):
                part = pl.ds(pl.multiple_of((chip * 2 + core) * share, share), share)
                target[k] = jnp.dot(
                    left, weights[:, part], preferred_element_type=jnp.float32
                ).astype(jnp.bfloat16)


def attend(where, queries, new_keys, new_values, cache_k, cache_v, lengths, out_proj):
    count, width = queries.shape
    length = cache_k.shape[1]
    share = out_proj.shape[1] // (2 * SIDE)
    shape = jax.ShapeDtypeStruct((SIDE, count, share), jnp.bfloat16)
    whole = pl.BlockSpec((SIDE, count, share), lambda i: (0, 0, 0))
    return pl.pallas_call(
        attend_kernel,
        grid=(count // BLOCK,),
        out_shape=(shape, shape),
        in_specs=[
            pl.BlockSpec(memory_space=pltpu.SMEM),
            pl.BlockSpec((BLOCK, width), lambda i: (i, 0)),
            pl.BlockSpec((BLOCK, HD), lambda i: (i, 0)),
            pl.BlockSpec((BLOCK, HD), lambda i: (i, 0)),
            pl.BlockSpec((BLOCK, length, HD), lambda i: (i, 0, 0)),
            pl.BlockSpec((BLOCK, length, HD), lambda i: (i, 0, 0)),
            pl.BlockSpec(memory_space=pltpu.SMEM),
            pl.BlockSpec(memory_space=pl.ANY),
        ],
        out_specs=(whole, whole),
        scratch_shapes=[
            pltpu.VMEM((count, width), jnp.bfloat16),
            pltpu.VMEM(out_proj.shape, jnp.bfloat16),
            pltpu.SemaphoreType.DMA(()),
        ],
        compiler_params=pltpu.CompilerParams(vmem_limit_bytes=VMEM),
        cost_estimate=pl.CostEstimate(
            flops=2 * count * width * out_proj.shape[1],
            bytes_accessed=4 * count * length * HD,
            transcendentals=0,
        ),
        name="attend_rows",
    )(where, queries, new_keys, new_values, cache_k, cache_v, lengths, out_proj)


def slot_codes(route_ids, experts, capacity):
    routes = route_ids.reshape(MICRO, MB, TOP)
    onehot = (routes[..., None] == jnp.arange(experts, dtype=jnp.int32)).astype(jnp.int32)
    flat = onehot.reshape(MICRO, MB * TOP, experts)
    before = jnp.cumsum(flat, axis=1) - flat
    slots = jnp.sum(before * flat, axis=-1).reshape(MICRO, MB, TOP)
    batch = jnp.arange(MICRO, dtype=jnp.int32)[:, None, None]
    return ((routes * MICRO + batch) * capacity + slots).reshape(MICRO * MB, TOP)


def body(
    resid,
    queries,
    new_keys,
    new_values,
    cache_k,
    cache_v,
    lengths,
    out_proj,
    norm_gain,
    router,
    route_ids,
    w_gate,
    w_up,
    w_down,
):
    count, model_width = resid.shape
    experts = router.shape[1]
    capacity = 4 * MB // experts
    slots = MICRO * capacity
    share = model_width // experts
    mine = lax.axis_index(EXPERT_AXES)
    where = jnp.stack([lax.axis_index("x"), lax.axis_index("c")]).astype(jnp.int32)

    own, others = attend(
        where, queries, new_keys, new_values, cache_k, cache_v, lengths, out_proj
    )
    arrived = lax.ppermute(others, "c", [(0, 1), (1, 0)])
    sums = [add(own[k], arrived[k]) for k in range(SIDE)]
    sums = [sums[0]] + [shift(sums[k], "x", k) for k in range(1, SIDE)]

    route_ids, _ = lax.optimization_barrier((route_ids, own))
    codes = slot_codes(route_ids, experts, capacity)
    places = jnp.arange(experts * slots, dtype=jnp.int32)[:, None]
    dispatch = ((codes[None, :, 0] == places) | (codes[None, :, 1] == places)).astype(jnp.bfloat16)
    slot = jnp.arange(slots, dtype=jnp.int32)[:, None]
    hits = [(c // slots == mine)[None] & (c % slots == slot) for c in (codes[:, 0], codes[:, 1])]
    own_dispatch = (hits[0] | hits[1]).astype(jnp.bfloat16)
    expert_ids = jnp.arange(experts, dtype=jnp.int32)
    match = jnp.sum((route_ids[:, :, None] == expert_ids).astype(jnp.bfloat16), axis=1)
    both = jnp.dot(own_dispatch, match, preferred_element_type=jnp.float32)
    own_mask = (expert_ids == mine)[None, :]

    state = lax.dynamic_slice_in_dim(resid, mine * share, share, 1).astype(jnp.float32)
    for one in sums:
        state = state + one.astype(jnp.float32)
    sent = jnp.dot(dispatch, state.astype(jnp.bfloat16), preferred_element_type=jnp.float32)
    sent = sent.astype(jnp.bfloat16).reshape(experts, slots, share)
    rows = lax.all_to_all(sent, EXPERT_AXES, 0, 0, tiled=True).astype(jnp.float32)
    mean_square = jnp.sum(rows * rows, axis=(0, 2)) / model_width
    gain = norm_gain.astype(jnp.float32).reshape(experts, 1, share)
    normed = (rows * lax.rsqrt(mean_square + epsilon)[None, :, None] * gain).astype(jnp.bfloat16)
    normed = normed.transpose(1, 0, 2).reshape(slots, model_width)

    logits = jnp.dot(normed, router, preferred_element_type=jnp.float32)
    own_logit = jnp.sum(jnp.where(own_mask, logits, 0.0), axis=1)
    other_logit = jnp.sum(jnp.where(own_mask, 0.0, logits * both), axis=1)
    gates = (1.0 / (1.0 + jnp.exp(other_logit - own_logit))).astype(jnp.bfloat16)

    def step(pair, turn):
        return ring(pair[0], "y", turn), ring(pair[1], "z", turn)

    def turn_over(pair, turn):
        return swap(pair[0], "z", turn), swap(pair[1], "y", turn)

    def join(left, right):
        return add(left[0], right[0]), add(left[1], right[1])

    start = (normed[:capacity], normed[capacity:])
    partner = turn_over(start, 0)
    near = tuple(jnp.concatenate(both, axis=0) for both in zip(start, partner))
    apart = turn_over(near, 1)
    whole = (4 * capacity,) * 2

    def pieces(one, two):
        return one[0], two[0], one[1], two[1]

    behind = step(near, 0), step(apart, 0)
    far = step(behind[0], 0), step(behind[1], 0)
    own_part, kept = expert_call(pieces(near, apart), whole, (w_gate, w_up, w_down), False)
    ahead = step(lay(pieces(near, apart), far[0]), 1)
    far_part, _ = expert_call(pieces(*far), whole, kept, True)
    far_sum = step(far_part, 1)
    behind_part, _ = expert_call(pieces(*behind), whole, kept, True, far_part)
    ahead_part, _ = expert_call(ahead, whole, kept, True)
    from_behind = step(ahead_part, 0)
    from_ahead = step(join(far_sum, behind_part), 1)

    def collect(side, axis):
        value = own_part[side].astype(jnp.float32) + from_behind[side].astype(jnp.float32)
        value = value + from_ahead[side].astype(jnp.float32)
        value = value.reshape(SIDE, capacity, model_width)
        sent = value[1:].astype(jnp.bfloat16)
        total = value[0] + swap(sent[0], axis, 0).astype(jnp.float32)
        total = total + swap(sent[1], axis, 1).astype(jnp.float32)
        return total + shift(sent[2], axis, 2).astype(jnp.float32)

    expert_out = jnp.concatenate([collect(0, "z"), collect(1, "y")], axis=0)

    weighted = (expert_out * gates.astype(jnp.float32)[:, None]).astype(jnp.bfloat16)
    weighted = weighted.reshape(slots, experts, share).transpose(1, 0, 2)
    back = lax.all_to_all(weighted, EXPERT_AXES, 0, 0, tiled=True)
    moe = lax.dot_general(
        dispatch,
        back.reshape(experts * slots, share),
        (((0,), (0,)), ((), ())),
        preferred_element_type=jnp.float32,
    )
    return (state + moe).astype(jnp.bfloat16)


def solution(mesh):
    fine = Mesh(mesh.devices.reshape(SIDE, SIDE, SIDE, 2), ("y", "z", "x", "c"))
    attn = ("y", "z")
    placed = (
        P(attn, None),
        P(attn, EXPERT_AXES),
        P(attn, EXPERT_AXES),
        P(attn, EXPERT_AXES),
        P(attn, None, EXPERT_AXES),
        P(attn, None, EXPERT_AXES),
        P(attn),
        P(EXPERT_AXES, None),
        P(),
        P(),
        P(attn, None),
        P(EXPERT_AXES, None, attn),
        P(EXPERT_AXES, None, attn),
        P(EXPERT_AXES, attn, None),
    )
    return jax.shard_map(
        body, mesh=fine, in_specs=placed, out_specs=P(attn, EXPERT_AXES), check_vma=False
    )
```

```python
import functools
import math

import jax
import jax.numpy as jnp
from jax import lax
from jax.experimental import pallas as pl
from jax.experimental.pallas import tpu as pltpu
from jax.sharding import Mesh
from jax.sharding import PartitionSpec as P

HD = 128
TOP = 2
MICRO = 2
MB = 32
SIDE = 4
EXPERT_AXES = ("x", "c")
DEEP = 8
WIDE = 6
BLOCK = 8
PARTS = 8
EXPERT_VMEM = 8 * 1024 * 1024
VMEM = 60 * 1024 * 1024

epsilon = 1e-05


def shift(value, axis, step):
    return lax.ppermute(value, axis, [(i, (i + step) % SIDE) for i in range(SIDE)])


def ring(value, axis, turn):
    perm = []
    for i in range(SIDE):
        for core in range(2):
            to = (i + (1 if core == turn else -1)) % SIDE
            perm.append((2 * i + core, 2 * to + core))
    return lax.ppermute(value, (axis, "c"), perm)


def swap(value, axis, turn):
    perm = []
    for i in range(SIDE):
        for core in range(2):
            partner = i ^ 1 if core == turn else SIDE - 1 - i
            perm.append((2 * i + core, 2 * partner + core))
    return lax.ppermute(value, (axis, "c"), perm)


def add(one, two):
    return (one.astype(jnp.float32) + two.astype(jnp.float32)).astype(jnp.bfloat16)


def expert_kernel(taken, given, kept, waits, *refs):
    sources, refs = refs[: len(taken)], refs[len(taken) :]
    weights, refs = refs[:3], refs[3 + waits :]
    targets, refs = refs[: len(given)], refs[len(given) :]
    if not kept:
        near, refs = refs[:3], refs[3:]
        weight_sems, refs = refs[-1], refs[:-1]
    rows, gate, upper, out, in_sems, out_sems = refs
    width = rows.shape[1]
    deep = width // DEEP
    wide = width // WIDE

    arrivals = []
    place = 0
    for index, (source, count) in enumerate(zip(sources, taken)):
        arrivals.append(
            pltpu.make_async_copy(source, rows.at[pl.ds(place, count)], in_sems.at[index])
        )
        place += count
    for copy in arrivals:
        copy.start()
    groups = [()] * (DEEP + WIDE)
    if not kept:
        groups = []
        for k in range(DEEP):
            part = pl.ds(k * deep, deep)
            groups.append(
                tuple(
                    pltpu.make_async_copy(
                        weights[w].at[0, part], near[w].at[part], weight_sems.at[2 * k + w]
                    )
                    for w in range(2)
                )
            )
        for n in range(WIDE):
            part = pl.ds(n * wide, wide)
            groups.append(
                (
                    pltpu.make_async_copy(
                        weights[2].at[0, :, part], near[2].at[:, part], weight_sems.at[2 * DEEP + n]
                    ),
                )
            )
        for group in groups:
            for copy in group:
                copy.start()
        weights = near
    w_gate, w_up, w_down = weights
    for copy in arrivals:
        copy.wait()

    for k in range(DEEP):
        for copy in groups[k]:
            copy.wait()
        part = pl.ds(k * deep, deep)
        more_gate = jnp.dot(rows[:, part], w_gate[part, :], preferred_element_type=jnp.float32)
        more_up = jnp.dot(rows[:, part], w_up[part, :], preferred_element_type=jnp.float32)
        if k == 0:
            gate[...] = more_gate
            upper[...] = more_up
        else:
            gate[...] += more_gate
            upper[...] += more_up
    value = gate[...]
    expanded = (value / (1.0 + jnp.exp(-value)) * upper[...]).astype(jnp.bfloat16)
    writes = []
    for n in range(WIDE):
        for copy in groups[DEEP + n]:
            copy.wait()
        part = pl.ds(n * wide, wide)
        out[:, part] = jnp.dot(
            expanded, w_down[:, part], preferred_element_type=jnp.float32
        ).astype(jnp.bfloat16)
        place = 0
        for index, (target, count) in enumerate(zip(targets, given)):
            write = pltpu.make_async_copy(
                out.at[pl.ds(place, count), part],
                target.at[:, part],
                out_sems.at[n * len(given) + index],
            )
            write.start()
            writes.append(write)
            place += count
    for write in writes:
        write.wait()


def expert_call(pieces, given, weights, kept, after=()):
    taken = tuple(p.shape[0] for p in pieces)
    total, width = sum(taken), pieces[0].shape[1]
    hidden = weights[2].shape[-2]
    anywhere = pl.BlockSpec(memory_space=pl.ANY)
    near = pl.BlockSpec(memory_space=pltpu.VMEM)
    outs = [jax.ShapeDtypeStruct((count, width), jnp.bfloat16) for count in given]
    scratch = [
        pltpu.VMEM((total, width), jnp.bfloat16),
        pltpu.VMEM((total, hidden), jnp.float32),
        pltpu.VMEM((total, hidden), jnp.float32),
        pltpu.VMEM((total, width), jnp.bfloat16),
        pltpu.SemaphoreType.DMA((len(taken),)),
        pltpu.SemaphoreType.DMA((len(given) * WIDE,)),
    ]
    if kept:
        weights = [pltpu.with_memory_space_constraint(w, pltpu.VMEM) for w in weights]
    else:
        weights = [pltpu.with_memory_space_constraint(w, pltpu.HBM) for w in weights]
        outs += [pltpu.VMEM(w.shape[1:], w.dtype) for w in weights]
        scratch.append(pltpu.SemaphoreType.DMA((2 * DEEP + WIDE,)))
    results = pl.pallas_call(
        functools.partial(expert_kernel, taken, given, kept, len(after)),
        out_shape=tuple(outs),
        in_specs=[anywhere] * len(taken)
        + [near if kept else anywhere] * 3
        + [anywhere] * len(after),
        out_specs=(anywhere,) * len(given) + (near,) * (len(outs) - len(given)),
        scratch_shapes=scratch,
        compiler_params=pltpu.CompilerParams(vmem_limit_bytes=EXPERT_VMEM),
        cost_estimate=pl.CostEstimate(flops=1000000, bytes_accessed=100000, transcendentals=0),
        name="expert_rows" if kept else "expert_rows_first",
    )(*pieces, *weights, *after)
    return results[: len(given)], results[len(given) :]


def lay_kernel(count, *refs):
    pieces, outs, sems = refs[:count], refs[-1 - count // 2 : -1], refs[-1]
    copies = []
    for index, piece in enumerate(pieces):
        rows = piece.shape[0]
        target = outs[index // 2].at[pl.ds(index % 2 * rows, rows)]
        copies.append(pltpu.make_async_copy(piece, target, sems.at[index]))
    for copy in copies:
        copy.start()
    for copy in copies:
        copy.wait()


def lay(pieces, after):
    anywhere = pl.BlockSpec(memory_space=pl.ANY)
    rows, width = pieces[0].shape
    shape = jax.ShapeDtypeStruct((2 * rows, width), pieces[0].dtype)
    return pl.pallas_call(
        functools.partial(lay_kernel, len(pieces)),
        out_shape=(shape,) * (len(pieces) // 2),
        in_specs=[anywhere] * (len(pieces) + len(after)),
        out_specs=(anywhere,) * (len(pieces) // 2),
        scratch_shapes=[pltpu.SemaphoreType.DMA((len(pieces),))],
        compiler_params=pltpu.CompilerParams(vmem_limit_bytes=1024 * 1024),
        cost_estimate=pl.CostEstimate(flops=1000, bytes_accessed=1000, transcendentals=0),
        name="lay_rows",
    )(*pieces, *after)


def attend_kernel(
    lengths, queries, new_keys, new_values, cache_k, cache_v, out_proj, mine, theirs, near_lengths, near_queries, near_keys, near_values, keys, values, heads, weights, sums, sems, out_sems
):
    count, length, _ = cache_k.shape
    share = mine.shape[2]
    width = queries.shape[1]
    group = width // HD
    blocks = count // BLOCK
    copies = []
    small = []
    for index, (source, target) in enumerate(
        (
            (lengths, near_lengths),
            (queries, near_queries),
            (new_keys, near_keys),
            (new_values, near_values),
        )
    ):
        small.append(pltpu.make_async_copy(source, target, sems.at[2 * blocks + PARTS + index]))
        small[-1].start()
    for g in range(blocks):
        part = pl.ds(g * BLOCK, BLOCK)
        copies.append(
            (
                pltpu.make_async_copy(cache_k.at[part], keys.at[part], sems.at[2 * g]),
                pltpu.make_async_copy(cache_v.at[part], values.at[part], sems.at[2 * g + 1]),
            )
        )
    rows = width // PARTS
    last = []
    for k in range(PARTS):
        part = pl.ds(k * rows, rows)
        last.append(
            pltpu.make_async_copy(out_proj.at[part], weights.at[part], sems.at[2 * blocks + k])
        )
    copies.append(tuple(last))
    for pair in copies:
        for copy in pair:
            copy.start()

    factor = 1.0 / math.sqrt(HD)
    lines = 8
    position = lax.broadcasted_iota(jnp.int32, (BLOCK, lines, length), 2)
    turn = lax.broadcasted_iota(jnp.int32, (BLOCK, lines, 1), 0)
    for copy in small:
        copy.wait()
    all_queries = near_queries[...].astype(jnp.float32)
    all_keys = near_keys[...].astype(jnp.float32)
    all_values = near_values[...].astype(jnp.float32)
    outs = []
    for g in range(blocks):
        rows = slice(g * BLOCK, (g + 1) * BLOCK)
        heads_in = [all_queries[rows, h * HD : (h + 1) * HD][:, None, :] for h in range(group)]
        empty = jnp.zeros((BLOCK, lines - group, HD), jnp.float32)
        query = jnp.concatenate(heads_in + [empty], axis=1)
        fresh_key = all_keys[rows][:, None, :]
        fresh_value = all_values[rows][:, None, :]
        used = jnp.zeros((BLOCK, lines, 1), jnp.int32)
        for r in range(BLOCK):
            used = jnp.where(turn == r, near_lengths[g * BLOCK + r], used)
        itself = jnp.sum(query * fresh_key, axis=2, keepdims=True) * factor
        for copy in copies[g]:
            copy.wait()
        scores = (
            jnp.einsum(
                "rhd,rld->rhl",
                query.astype(jnp.bfloat16),
                keys[rows],
                preferred_element_type=jnp.float32,
            )
            * factor
        )
        masked = jnp.where(position < used, scores, -jnp.inf)
        highest = jnp.maximum(jnp.max(masked, axis=2, keepdims=True), itself)
        spread = jnp.exp(masked - highest)
        own_exp = jnp.exp(itself - highest)
        inverse = 1.0 / (jnp.sum(spread, axis=2, keepdims=True) + own_exp)
        probs = (spread * inverse).astype(jnp.bfloat16)
        own_prob = (own_exp * inverse).astype(jnp.bfloat16).astype(jnp.float32)
        mixed = jnp.einsum(
            "rhl,rld->rhd", probs, values[rows], preferred_element_type=jnp.float32
        )
        mixed = mixed + own_prob * fresh_value
        outs.append(jnp.concatenate([mixed[:, h, :] for h in range(group)], axis=1))
        if g % 2 == 1:
            heads[pl.ds((g - 1) * BLOCK, 2 * BLOCK), :] = jnp.concatenate(
                outs[-2:], axis=0
            ).astype(jnp.bfloat16)

    for copy in copies[-1]:
        copy.wait()
    left = heads[...]
    chip_here, core_here = lax.axis_index("x"), lax.axis_index("c")
    writes = []
    for side, (core, target) in enumerate(((1 - core_here, theirs), (core_here, mine))):
        for k in range(SIDE):
            chip = lax.rem(chip_here + k, SIDE)
            part = pl.ds(pl.multiple_of((chip * 2 + core) * share, share), share)
            place = side * SIDE + k
            sums[place] = jnp.dot(
                left, weights[:, part], preferred_element_type=jnp.float32
            ).astype(jnp.bfloat16)
            writes.append(
                pltpu.make_async_copy(sums.at[place], target.at[k], out_sems.at[place])
            )
            writes[-1].start()
    for write in writes:
        write.wait()


def attend(queries, new_keys, new_values, cache_k, cache_v, lengths, out_proj):
    count, width = queries.shape
    length = cache_k.shape[1]
    share = out_proj.shape[1] // (2 * SIDE)
    shape = jax.ShapeDtypeStruct((SIDE, count, share), jnp.bfloat16)
    anywhere = pl.BlockSpec(memory_space=pl.ANY)
    return pl.pallas_call(
        attend_kernel,
        out_shape=(shape, shape),
        in_specs=[anywhere] * 7,
        out_specs=(anywhere, anywhere),
        scratch_shapes=[
            pltpu.SMEM(lengths.shape, jnp.int32),
            pltpu.VMEM(queries.shape, jnp.bfloat16),
            pltpu.VMEM(new_keys.shape, jnp.bfloat16),
            pltpu.VMEM(new_values.shape, jnp.bfloat16),
            pltpu.VMEM(cache_k.shape, jnp.bfloat16),
            pltpu.VMEM(cache_v.shape, jnp.bfloat16),
            pltpu.VMEM((count, width), jnp.bfloat16),
            pltpu.VMEM(out_proj.shape, jnp.bfloat16),
            pltpu.VMEM((2 * SIDE, count, share), jnp.bfloat16),
            pltpu.SemaphoreType.DMA((2 * count // BLOCK + PARTS + 4,)),
            pltpu.SemaphoreType.DMA((2 * SIDE,)),
        ],
        compiler_params=pltpu.CompilerParams(vmem_limit_bytes=VMEM),
        cost_estimate=pl.CostEstimate(
            flops=2 * count * width * out_proj.shape[1],
            bytes_accessed=4 * count * length * HD,
            transcendentals=0,
        ),
        name="attend_rows",
    )(lengths, queries, new_keys, new_values, cache_k, cache_v, out_proj)


def slot_codes(route_ids, experts, capacity):
    routes = route_ids.reshape(MICRO, MB, TOP)
    onehot = (routes[..., None] == jnp.arange(experts, dtype=jnp.int32)).astype(jnp.int32)
    flat = onehot.reshape(MICRO, MB * TOP, experts)
    before = jnp.cumsum(flat, axis=1) - flat
    slots = jnp.sum(before * flat, axis=-1).reshape(MICRO, MB, TOP)
    batch = jnp.arange(MICRO, dtype=jnp.int32)[:, None, None]
    return ((routes * MICRO + batch) * capacity + slots).reshape(MICRO * MB, TOP)


def body(
    resid,
    queries,
    new_keys,
    new_values,
    cache_k,
    cache_v,
    lengths,
    out_proj,
    norm_gain,
    router,
    route_ids,
    w_gate,
    w_up,
    w_down,
):
    count, model_width = resid.shape
    experts = router.shape[1]
    capacity = 4 * MB // experts
    slots = MICRO * capacity
    share = model_width // experts
    mine = lax.axis_index(EXPERT_AXES)

    own, others = attend(queries, new_keys, new_values, cache_k, cache_v, lengths, out_proj)
    arrived = lax.ppermute(others, "c", [(0, 1), (1, 0)])
    sums = [add(own[k], arrived[k]) for k in range(SIDE)]
    sums = [sums[0]] + [shift(sums[k], "x", k) for k in range(1, SIDE)]

    route_ids, _ = lax.optimization_barrier((route_ids, own))
    codes = slot_codes(route_ids, experts, capacity)
    places = jnp.arange(experts * slots, dtype=jnp.int32)[:, None]
    dispatch = ((codes[None, :, 0] == places) | (codes[None, :, 1] == places)).astype(jnp.bfloat16)
    slot = jnp.arange(slots, dtype=jnp.int32)[:, None]
    hits = [(c // slots == mine)[None] & (c % slots == slot) for c in (codes[:, 0], codes[:, 1])]
    own_dispatch = (hits[0] | hits[1]).astype(jnp.bfloat16)
    expert_ids = jnp.arange(experts, dtype=jnp.int32)
    match = jnp.sum((route_ids[:, :, None] == expert_ids).astype(jnp.bfloat16), axis=1)
    both = jnp.dot(own_dispatch, match, preferred_element_type=jnp.float32)
    own_mask = (expert_ids == mine)[None, :]

    state = lax.dynamic_slice_in_dim(resid, mine * share, share, 1).astype(jnp.float32)
    for one in sums:
        state = state + one.astype(jnp.float32)
    sent = jnp.dot(dispatch, state.astype(jnp.bfloat16), preferred_element_type=jnp.float32)
    sent = sent.astype(jnp.bfloat16).reshape(experts, slots, share)
    rows = lax.all_to_all(sent, EXPERT_AXES, 0, 0, tiled=True).astype(jnp.float32)
    mean_square = jnp.sum(rows * rows, axis=(0, 2)) / model_width
    gain = norm_gain.astype(jnp.float32).reshape(experts, 1, share)
    normed = (rows * lax.rsqrt(mean_square + epsilon)[None, :, None] * gain).astype(jnp.bfloat16)
    normed = normed.transpose(1, 0, 2).reshape(slots, model_width)

    logits = jnp.dot(normed, router, preferred_element_type=jnp.float32)
    own_logit = jnp.sum(jnp.where(own_mask, logits, 0.0), axis=1)
    other_logit = jnp.sum(jnp.where(own_mask, 0.0, logits * both), axis=1)
    gates = (1.0 / (1.0 + jnp.exp(other_logit - own_logit))).astype(jnp.bfloat16)

    def step(pair, turn):
        return ring(pair[0], "y", turn), ring(pair[1], "z", turn)

    def turn_over(pair, turn):
        return swap(pair[0], "z", turn), swap(pair[1], "y", turn)

    def join(left, right):
        return add(left[0], right[0]), add(left[1], right[1])

    start = (normed[:capacity], normed[capacity:])
    partner = turn_over(start, 0)
    near = tuple(jnp.concatenate(both, axis=0) for both in zip(start, partner))
    apart = turn_over(near, 1)
    whole = (4 * capacity,) * 2

    def pieces(one, two):
        return one[0], two[0], one[1], two[1]

    behind = step(near, 0), step(apart, 0)
    far = step(behind[0], 0), step(behind[1], 0)
    own_part, kept = expert_call(pieces(near, apart), whole, (w_gate, w_up, w_down), False)
    ahead = step(lay(pieces(near, apart), far[0]), 1)
    far_part, _ = expert_call(pieces(*far), whole, kept, True)
    far_sum = step(far_part, 1)
    behind_part, _ = expert_call(pieces(*behind), whole, kept, True, far_part)
    ahead_part, _ = expert_call(ahead, whole, kept, True)
    from_behind = step(ahead_part, 0)
    from_ahead = step(join(far_sum, behind_part), 1)

    def collect(side, axis):
        value = own_part[side].astype(jnp.float32) + from_behind[side].astype(jnp.float32)
        value = value + from_ahead[side].astype(jnp.float32)
        value = value.reshape(SIDE, capacity, model_width)
        sent = value[1:].astype(jnp.bfloat16)
        total = value[0] + swap(sent[0], axis, 0).astype(jnp.float32)
        total = total + swap(sent[1], axis, 1).astype(jnp.float32)
        return total + shift(sent[2], axis, 2).astype(jnp.float32)

    expert_out = jnp.concatenate([collect(0, "z"), collect(1, "y")], axis=0)

    weighted = (expert_out * gates.astype(jnp.float32)[:, None]).astype(jnp.bfloat16)
    weighted = weighted.reshape(slots, experts, share).transpose(1, 0, 2)
    back = lax.all_to_all(weighted, EXPERT_AXES, 0, 0, tiled=True)
    moe = lax.dot_general(
        dispatch,
        back.reshape(experts * slots, share),
        (((0,), (0,)), ((), ())),
        preferred_element_type=jnp.float32,
    )
    return (state + moe).astype(jnp.bfloat16)


def solution(mesh):
    fine = Mesh(mesh.devices.reshape(SIDE, SIDE, SIDE, 2), ("y", "z", "x", "c"))
    attn = ("y", "z")
    placed = (
        P(attn, None),
        P(attn, EXPERT_AXES),
        P(attn, EXPERT_AXES),
        P(attn, EXPERT_AXES),
        P(attn, None, EXPERT_AXES),
        P(attn, None, EXPERT_AXES),
        P(attn),
        P(EXPERT_AXES, None),
        P(),
        P(),
        P(attn, None),
        P(EXPERT_AXES, None, attn),
        P(EXPERT_AXES, None, attn),
        P(EXPERT_AXES, attn, None),
    )
    return jax.shard_map(
        body, mesh=fine, in_specs=placed, out_specs=P(attn, EXPERT_AXES), check_vma=False
    )
```

```python
import functools
import math

import jax
import jax.numpy as jnp
from jax import lax
from jax.experimental import pallas as pl
from jax.experimental.pallas import tpu as pltpu
from jax.sharding import Mesh
from jax.sharding import PartitionSpec as P

HD = 128
TOP = 2
MICRO = 2
MB = 32
SIDE = 4
EXPERT_AXES = ("x", "c")
DEEP = 8
WIDE = 6
BLOCK = 16
PARTS = 8
EXPERT_VMEM = 8 * 1024 * 1024
VMEM = 60 * 1024 * 1024

epsilon = 1e-05


def shift(value, axis, step):
    return lax.ppermute(value, axis, [(i, (i + step) % SIDE) for i in range(SIDE)])


def ring(value, axis, turn):
    perm = []
    for i in range(SIDE):
        for core in range(2):
            to = (i + (1 if core == turn else -1)) % SIDE
            perm.append((2 * i + core, 2 * to + core))
    return lax.ppermute(value, (axis, "c"), perm)


def swap(value, axis, turn):
    perm = []
    for i in range(SIDE):
        for core in range(2):
            partner = i ^ 1 if core == turn else SIDE - 1 - i
            perm.append((2 * i + core, 2 * partner + core))
    return lax.ppermute(value, (axis, "c"), perm)


def add(one, two):
    return (one.astype(jnp.float32) + two.astype(jnp.float32)).astype(jnp.bfloat16)


def expert_kernel(taken, given, kept, waits, *refs):
    sources, refs = refs[: len(taken)], refs[len(taken) :]
    weights, refs = refs[:3], refs[3 + waits :]
    targets, refs = refs[: len(given)], refs[len(given) :]
    if not kept:
        near, refs = refs[:3], refs[3:]
        weight_sems, refs = refs[-1], refs[:-1]
    rows, gate, upper, out, in_sems, out_sems = refs
    width = rows.shape[1]
    deep = width // DEEP
    wide = width // WIDE

    arrivals = []
    place = 0
    for index, (source, count) in enumerate(zip(sources, taken)):
        arrivals.append(
            pltpu.make_async_copy(source, rows.at[pl.ds(place, count)], in_sems.at[index])
        )
        place += count
    for copy in arrivals:
        copy.start()
    groups = [()] * (DEEP + WIDE)
    if not kept:
        groups = []
        for k in range(DEEP):
            part = pl.ds(k * deep, deep)
            groups.append(
                tuple(
                    pltpu.make_async_copy(
                        weights[w].at[0, part], near[w].at[part], weight_sems.at[2 * k + w]
                    )
                    for w in range(2)
                )
            )
        for n in range(WIDE):
            part = pl.ds(n * wide, wide)
            groups.append(
                (
                    pltpu.make_async_copy(
                        weights[2].at[0, :, part], near[2].at[:, part], weight_sems.at[2 * DEEP + n]
                    ),
                )
            )
        for group in groups:
            for copy in group:
                copy.start()
        weights = near
    w_gate, w_up, w_down = weights
    for copy in arrivals:
        copy.wait()

    for k in range(DEEP):
        for copy in groups[k]:
            copy.wait()
        part = pl.ds(k * deep, deep)
        more_gate = jnp.dot(rows[:, part], w_gate[part, :], preferred_element_type=jnp.float32)
        more_up = jnp.dot(rows[:, part], w_up[part, :], preferred_element_type=jnp.float32)
        if k == 0:
            gate[...] = more_gate
            upper[...] = more_up
        else:
            gate[...] += more_gate
            upper[...] += more_up
    value = gate[...]
    expanded = (value / (1.0 + jnp.exp(-value)) * upper[...]).astype(jnp.bfloat16)
    writes = []
    for n in range(WIDE):
        for copy in groups[DEEP + n]:
            copy.wait()
        part = pl.ds(n * wide, wide)
        out[:, part] = jnp.dot(
            expanded, w_down[:, part], preferred_element_type=jnp.float32
        ).astype(jnp.bfloat16)
        place = 0
        for index, (target, count) in enumerate(zip(targets, given)):
            write = pltpu.make_async_copy(
                out.at[pl.ds(place, count), part],
                target.at[:, part],
                out_sems.at[n * len(given) + index],
            )
            write.start()
            writes.append(write)
            place += count
    for write in writes:
        write.wait()


def expert_call(pieces, given, weights, kept, after=()):
    taken = tuple(p.shape[0] for p in pieces)
    total, width = sum(taken), pieces[0].shape[1]
    hidden = weights[2].shape[-2]
    anywhere = pl.BlockSpec(memory_space=pl.ANY)
    near = pl.BlockSpec(memory_space=pltpu.VMEM)
    outs = [jax.ShapeDtypeStruct((count, width), jnp.bfloat16) for count in given]
    scratch = [
        pltpu.VMEM((total, width), jnp.bfloat16),
        pltpu.VMEM((total, hidden), jnp.float32),
        pltpu.VMEM((total, hidden), jnp.float32),
        pltpu.VMEM((total, width), jnp.bfloat16),
        pltpu.SemaphoreType.DMA((len(taken),)),
        pltpu.SemaphoreType.DMA((len(given) * WIDE,)),
    ]
    if kept:
        weights = [pltpu.with_memory_space_constraint(w, pltpu.VMEM) for w in weights]
    else:
        weights = [pltpu.with_memory_space_constraint(w, pltpu.HBM) for w in weights]
        outs += [pltpu.VMEM(w.shape[1:], w.dtype) for w in weights]
        scratch.append(pltpu.SemaphoreType.DMA((2 * DEEP + WIDE,)))
    results = pl.pallas_call(
        functools.partial(expert_kernel, taken, given, kept, len(after)),
        out_shape=tuple(outs),
        in_specs=[anywhere] * len(taken)
        + [near if kept else anywhere] * 3
        + [anywhere] * len(after),
        out_specs=(anywhere,) * len(given) + (near,) * (len(outs) - len(given)),
        scratch_shapes=scratch,
        compiler_params=pltpu.CompilerParams(vmem_limit_bytes=EXPERT_VMEM),
        cost_estimate=pl.CostEstimate(flops=1000000, bytes_accessed=100000, transcendentals=0),
        name="expert_rows" if kept else "expert_rows_first",
    )(*pieces, *weights, *after)
    return results[: len(given)], results[len(given) :]


def lay_kernel(count, *refs):
    pieces, outs, sems = refs[:count], refs[-1 - count // 2 : -1], refs[-1]
    copies = []
    for index, piece in enumerate(pieces):
        rows = piece.shape[0]
        target = outs[index // 2].at[pl.ds(index % 2 * rows, rows)]
        copies.append(pltpu.make_async_copy(piece, target, sems.at[index]))
    for copy in copies:
        copy.start()
    for copy in copies:
        copy.wait()


def lay(pieces, after):
    anywhere = pl.BlockSpec(memory_space=pl.ANY)
    rows, width = pieces[0].shape
    shape = jax.ShapeDtypeStruct((2 * rows, width), pieces[0].dtype)
    return pl.pallas_call(
        functools.partial(lay_kernel, len(pieces)),
        out_shape=(shape,) * (len(pieces) // 2),
        in_specs=[anywhere] * (len(pieces) + len(after)),
        out_specs=(anywhere,) * (len(pieces) // 2),
        scratch_shapes=[pltpu.SemaphoreType.DMA((len(pieces),))],
        compiler_params=pltpu.CompilerParams(vmem_limit_bytes=1024 * 1024),
        cost_estimate=pl.CostEstimate(flops=1000, bytes_accessed=1000, transcendentals=0),
        name="lay_rows",
    )(*pieces, *after)


def attend_kernel(
    lengths, queries, new_keys, new_values, cache_k, cache_v, out_proj, mine, theirs, near_lengths, near_queries, near_keys, near_values, keys, values, heads, weights, sums, sems, out_sems
):
    count, length, _ = cache_k.shape
    share = mine.shape[2]
    width = queries.shape[1]
    group = width // HD
    blocks = count // BLOCK
    copies = []
    small = []
    for index, (source, target) in enumerate(
        (
            (lengths, near_lengths),
            (queries, near_queries),
            (new_keys, near_keys),
            (new_values, near_values),
        )
    ):
        small.append(pltpu.make_async_copy(source, target, sems.at[2 * blocks + PARTS + index]))
        small[-1].start()
    for g in range(blocks):
        part = pl.ds(g * BLOCK, BLOCK)
        copies.append(
            (
                pltpu.make_async_copy(cache_k.at[part], keys.at[part], sems.at[2 * g]),
                pltpu.make_async_copy(cache_v.at[part], values.at[part], sems.at[2 * g + 1]),
            )
        )
    rows = width // PARTS
    last = []
    for k in range(PARTS):
        part = pl.ds(k * rows, rows)
        last.append(
            pltpu.make_async_copy(out_proj.at[part], weights.at[part], sems.at[2 * blocks + k])
        )
    copies.append(tuple(last))
    for pair in copies:
        for copy in pair:
            copy.start()

    factor = 1.0 / math.sqrt(HD)
    lines = 8
    position = lax.broadcasted_iota(jnp.int32, (BLOCK, lines, length), 2)
    turn = lax.broadcasted_iota(jnp.int32, (BLOCK, lines, 1), 0)
    for copy in small:
        copy.wait()
    all_queries = near_queries[...].astype(jnp.float32)
    all_keys = near_keys[...].astype(jnp.float32)
    all_values = near_values[...].astype(jnp.float32)
    outs = []
    for g in range(blocks):
        rows = slice(g * BLOCK, (g + 1) * BLOCK)
        heads_in = [all_queries[rows, h * HD : (h + 1) * HD][:, None, :] for h in range(group)]
        empty = jnp.zeros((BLOCK, lines - group, HD), jnp.float32)
        query = jnp.concatenate(heads_in + [empty], axis=1)
        fresh_key = all_keys[rows][:, None, :]
        fresh_value = all_values[rows][:, None, :]
        used = jnp.zeros((BLOCK, lines, 1), jnp.int32)
        for r in range(BLOCK):
            used = jnp.where(turn == r, near_lengths[g * BLOCK + r], used)
        itself = jnp.sum(query * fresh_key, axis=2, keepdims=True) * factor
        for copy in copies[g]:
            copy.wait()
        scores = (
            jnp.einsum(
                "rhd,rld->rhl",
                query.astype(jnp.bfloat16),
                keys[rows],
                preferred_element_type=jnp.float32,
            )
            * factor
        )
        masked = jnp.where(position < used, scores, -jnp.inf)
        highest = jnp.maximum(jnp.max(masked, axis=2, keepdims=True), itself)
        spread = jnp.exp(masked - highest)
        own_exp = jnp.exp(itself - highest)
        inverse = 1.0 / (jnp.sum(spread, axis=2, keepdims=True) + own_exp)
        probs = (spread * inverse).astype(jnp.bfloat16)
        own_prob = (own_exp * inverse).astype(jnp.bfloat16).astype(jnp.float32)
        mixed = jnp.einsum(
            "rhl,rld->rhd", probs, values[rows], preferred_element_type=jnp.float32
        )
        mixed = mixed + own_prob * fresh_value
        outs.append(jnp.concatenate([mixed[:, h, :] for h in range(group)], axis=1))
        if g % 2 == 1:
            heads[pl.ds((g - 1) * BLOCK, 2 * BLOCK), :] = jnp.concatenate(
                outs[-2:], axis=0
            ).astype(jnp.bfloat16)

    for copy in copies[-1]:
        copy.wait()
    left = heads[...]
    chip_here, core_here = lax.axis_index("x"), lax.axis_index("c")
    writes = []
    for side, (core, target) in enumerate(((1 - core_here, theirs), (core_here, mine))):
        for k in range(SIDE):
            chip = lax.rem(chip_here + k, SIDE)
            part = pl.ds(pl.multiple_of((chip * 2 + core) * share, share), share)
            place = side * SIDE + k
            sums[place] = jnp.dot(
                left, weights[:, part], preferred_element_type=jnp.float32
            ).astype(jnp.bfloat16)
            writes.append(
                pltpu.make_async_copy(sums.at[place], target.at[k], out_sems.at[place])
            )
            writes[-1].start()
    for write in writes:
        write.wait()


def attend(queries, new_keys, new_values, cache_k, cache_v, lengths, out_proj):
    count, width = queries.shape
    length = cache_k.shape[1]
    share = out_proj.shape[1] // (2 * SIDE)
    shape = jax.ShapeDtypeStruct((SIDE, count, share), jnp.bfloat16)
    anywhere = pl.BlockSpec(memory_space=pl.ANY)
    return pl.pallas_call(
        attend_kernel,
        out_shape=(shape, shape),
        in_specs=[anywhere] * 7,
        out_specs=(anywhere, anywhere),
        scratch_shapes=[
            pltpu.SMEM(lengths.shape, jnp.int32),
            pltpu.VMEM(queries.shape, jnp.bfloat16),
            pltpu.VMEM(new_keys.shape, jnp.bfloat16),
            pltpu.VMEM(new_values.shape, jnp.bfloat16),
            pltpu.VMEM(cache_k.shape, jnp.bfloat16),
            pltpu.VMEM(cache_v.shape, jnp.bfloat16),
            pltpu.VMEM((count, width), jnp.bfloat16),
            pltpu.VMEM(out_proj.shape, jnp.bfloat16),
            pltpu.VMEM((2 * SIDE, count, share), jnp.bfloat16),
            pltpu.SemaphoreType.DMA((2 * count // BLOCK + PARTS + 4,)),
            pltpu.SemaphoreType.DMA((2 * SIDE,)),
        ],
        compiler_params=pltpu.CompilerParams(vmem_limit_bytes=VMEM),
        cost_estimate=pl.CostEstimate(
            flops=2 * count * width * out_proj.shape[1],
            bytes_accessed=4 * count * length * HD,
            transcendentals=0,
        ),
        name="attend_rows",
    )(lengths, queries, new_keys, new_values, cache_k, cache_v, out_proj)


def slot_codes(route_ids, experts, capacity):
    routes = route_ids.reshape(MICRO, MB, TOP)
    onehot = (routes[..., None] == jnp.arange(experts, dtype=jnp.int32)).astype(jnp.int32)
    flat = onehot.reshape(MICRO, MB * TOP, experts)
    before = jnp.cumsum(flat, axis=1) - flat
    slots = jnp.sum(before * flat, axis=-1).reshape(MICRO, MB, TOP)
    batch = jnp.arange(MICRO, dtype=jnp.int32)[:, None, None]
    return ((routes * MICRO + batch) * capacity + slots).reshape(MICRO * MB, TOP)


def body(
    resid,
    queries,
    new_keys,
    new_values,
    cache_k,
    cache_v,
    lengths,
    out_proj,
    norm_gain,
    router,
    route_ids,
    w_gate,
    w_up,
    w_down,
):
    count, model_width = resid.shape
    experts = router.shape[1]
    capacity = 4 * MB // experts
    slots = MICRO * capacity
    share = model_width // experts
    mine = lax.axis_index(EXPERT_AXES)

    own, others = attend(queries, new_keys, new_values, cache_k, cache_v, lengths, out_proj)
    arrived = lax.ppermute(others, "c", [(0, 1), (1, 0)])
    sums = [add(own[k], arrived[k]) for k in range(SIDE)]
    sums = [sums[0]] + [shift(sums[k], "x", k) for k in range(1, SIDE)]

    route_ids, _ = lax.optimization_barrier((route_ids, own))
    codes = slot_codes(route_ids, experts, capacity)
    places = jnp.arange(experts * slots, dtype=jnp.int32)[:, None]
    dispatch = ((codes[None, :, 0] == places) | (codes[None, :, 1] == places)).astype(jnp.bfloat16)
    slot = jnp.arange(slots, dtype=jnp.int32)[:, None]
    hits = [(c // slots == mine)[None] & (c % slots == slot) for c in (codes[:, 0], codes[:, 1])]
    own_dispatch = (hits[0] | hits[1]).astype(jnp.bfloat16)
    expert_ids = jnp.arange(experts, dtype=jnp.int32)
    match = jnp.sum((route_ids[:, :, None] == expert_ids).astype(jnp.bfloat16), axis=1)
    both = jnp.dot(own_dispatch, match, preferred_element_type=jnp.float32)
    own_mask = (expert_ids == mine)[None, :]

    state = lax.dynamic_slice_in_dim(resid, mine * share, share, 1).astype(jnp.float32)
    for one in sums:
        state = state + one.astype(jnp.float32)
    sent = jnp.dot(dispatch, state.astype(jnp.bfloat16), preferred_element_type=jnp.float32)
    sent = sent.astype(jnp.bfloat16).reshape(experts, slots, share)
    rows = lax.all_to_all(sent, EXPERT_AXES, 0, 0, tiled=True).astype(jnp.float32)
    mean_square = jnp.sum(rows * rows, axis=(0, 2)) / model_width
    gain = norm_gain.astype(jnp.float32).reshape(experts, 1, share)
    normed = (rows * lax.rsqrt(mean_square + epsilon)[None, :, None] * gain).astype(jnp.bfloat16)
    normed = normed.transpose(1, 0, 2).reshape(slots, model_width)

    logits = jnp.dot(normed, router, preferred_element_type=jnp.float32)
    own_logit = jnp.sum(jnp.where(own_mask, logits, 0.0), axis=1)
    other_logit = jnp.sum(jnp.where(own_mask, 0.0, logits * both), axis=1)
    gates = (1.0 / (1.0 + jnp.exp(other_logit - own_logit))).astype(jnp.bfloat16)

    def step(pair, turn):
        return ring(pair[0], "y", turn), ring(pair[1], "z", turn)

    def turn_over(pair, turn):
        return swap(pair[0], "z", turn), swap(pair[1], "y", turn)

    def join(left, right):
        return add(left[0], right[0]), add(left[1], right[1])

    start = (normed[:capacity], normed[capacity:])
    partner = turn_over(start, 0)
    near = tuple(jnp.concatenate(both, axis=0) for both in zip(start, partner))
    apart = turn_over(near, 1)
    whole = (4 * capacity,) * 2

    def pieces(one, two):
        return one[0], two[0], one[1], two[1]

    behind = step(near, 0), step(apart, 0)
    far = step(behind[0], 0), step(behind[1], 0)
    own_part, kept = expert_call(pieces(near, apart), whole, (w_gate, w_up, w_down), False)
    ahead = step(lay(pieces(near, apart), far[0]), 1)
    far_part, _ = expert_call(pieces(*far), whole, kept, True)
    far_sum = step(far_part, 1)
    behind_part, _ = expert_call(pieces(*behind), whole, kept, True, far_part)
    ahead_part, _ = expert_call(ahead, whole, kept, True)
    from_behind = step(ahead_part, 0)
    from_ahead = step(join(far_sum, behind_part), 1)

    def collect(side, axis):
        value = own_part[side].astype(jnp.float32) + from_behind[side].astype(jnp.float32)
        value = value + from_ahead[side].astype(jnp.float32)
        value = value.reshape(SIDE, capacity, model_width)
        sent = value[1:].astype(jnp.bfloat16)
        total = value[0] + swap(sent[0], axis, 0).astype(jnp.float32)
        total = total + swap(sent[1], axis, 1).astype(jnp.float32)
        return total + shift(sent[2], axis, 2).astype(jnp.float32)

    expert_out = jnp.concatenate([collect(0, "z"), collect(1, "y")], axis=0)

    weighted = (expert_out * gates.astype(jnp.float32)[:, None]).astype(jnp.bfloat16)
    weighted = weighted.reshape(slots, experts, share).transpose(1, 0, 2)
    back = lax.all_to_all(weighted, EXPERT_AXES, 0, 0, tiled=True)
    moe = lax.dot_general(
        dispatch,
        back.reshape(experts * slots, share),
        (((0,), (0,)), ((), ())),
        preferred_element_type=jnp.float32,
    )
    return (state + moe).astype(jnp.bfloat16)


def solution(mesh):
    fine = Mesh(mesh.devices.reshape(SIDE, SIDE, SIDE, 2), ("y", "z", "x", "c"))
    attn = ("y", "z")
    placed = (
        P(attn, None),
        P(attn, EXPERT_AXES),
        P(attn, EXPERT_AXES),
        P(attn, EXPERT_AXES),
        P(attn, None, EXPERT_AXES),
        P(attn, None, EXPERT_AXES),
        P(attn),
        P(EXPERT_AXES, None),
        P(),
        P(),
        P(attn, None),
        P(EXPERT_AXES, None, attn),
        P(EXPERT_AXES, None, attn),
        P(EXPERT_AXES, attn, None),
    )
    return jax.shard_map(
        body, mesh=fine, in_specs=placed, out_specs=P(attn, EXPERT_AXES), check_vma=False
    )
```

```python
import functools
import math

import jax
import jax.numpy as jnp
from jax import lax
from jax.experimental import pallas as pl
from jax.experimental.pallas import tpu as pltpu
from jax.sharding import Mesh
from jax.sharding import PartitionSpec as P

HD = 128
TOP = 2
MICRO = 2
MB = 32
SIDE = 4
EXPERT_AXES = ("x", "c")
DEEP = 8
WIDE = 6
BLOCK = 16
PARTS = 8
EXPERT_VMEM = 8 * 1024 * 1024
VMEM = 60 * 1024 * 1024

epsilon = 1e-05


def shift(value, axis, step):
    return lax.ppermute(value, axis, [(i, (i + step) % SIDE) for i in range(SIDE)])


def ring(value, axis, turn):
    perm = []
    for i in range(SIDE):
        for core in range(2):
            to = (i + (1 if core == turn else -1)) % SIDE
            perm.append((2 * i + core, 2 * to + core))
    return lax.ppermute(value, (axis, "c"), perm)


def swap(value, axis, turn):
    perm = []
    for i in range(SIDE):
        for core in range(2):
            partner = i ^ 1 if core == turn else SIDE - 1 - i
            perm.append((2 * i + core, 2 * partner + core))
    return lax.ppermute(value, (axis, "c"), perm)


def add(one, two):
    return (one.astype(jnp.float32) + two.astype(jnp.float32)).astype(jnp.bfloat16)


def expert_kernel(taken, given, kept, waits, *refs):
    sources, refs = refs[: len(taken)], refs[len(taken) :]
    weights, refs = refs[:3], refs[3 + waits :]
    targets, refs = refs[: len(given)], refs[len(given) :]
    if not kept:
        near, refs = refs[:3], refs[3:]
        weight_sems, refs = refs[-1], refs[:-1]
    rows, gate, upper, out, in_sems, out_sems = refs
    width = rows.shape[1]
    deep = width // DEEP
    wide = width // WIDE

    arrivals = []
    place = 0
    for index, (source, count) in enumerate(zip(sources, taken)):
        for k in range(DEEP):
            part = pl.ds(k * deep, deep)
            arrivals.append(
                pltpu.make_async_copy(
                    source.at[:, part],
                    rows.at[pl.ds(place, count), part],
                    in_sems.at[index * DEEP + k],
                )
            )
        place += count
    for k in range(DEEP):
        for copy in arrivals[k::DEEP]:
            copy.start()
    groups = [()] * (DEEP + WIDE)
    if not kept:
        groups = []
        for k in range(DEEP):
            part = pl.ds(k * deep, deep)
            groups.append(
                tuple(
                    pltpu.make_async_copy(
                        weights[w].at[0, part], near[w].at[part], weight_sems.at[2 * k + w]
                    )
                    for w in range(2)
                )
            )
        for n in range(WIDE):
            part = pl.ds(n * wide, wide)
            groups.append(
                (
                    pltpu.make_async_copy(
                        weights[2].at[0, :, part], near[2].at[:, part], weight_sems.at[2 * DEEP + n]
                    ),
                )
            )
        for group in groups:
            for copy in group:
                copy.start()
        weights = near
    w_gate, w_up, w_down = weights

    for k in range(DEEP):
        for copy in arrivals[k::DEEP]:
            copy.wait()
        for copy in groups[k]:
            copy.wait()
        part = pl.ds(k * deep, deep)
        more_gate = jnp.dot(rows[:, part], w_gate[part, :], preferred_element_type=jnp.float32)
        more_up = jnp.dot(rows[:, part], w_up[part, :], preferred_element_type=jnp.float32)
        if k == 0:
            gate[...] = more_gate
            upper[...] = more_up
        else:
            gate[...] += more_gate
            upper[...] += more_up
    value = gate[...]
    expanded = (value / (1.0 + jnp.exp(-value)) * upper[...]).astype(jnp.bfloat16)
    writes = []
    for n in range(WIDE):
        for copy in groups[DEEP + n]:
            copy.wait()
        part = pl.ds(n * wide, wide)
        out[:, part] = jnp.dot(
            expanded, w_down[:, part], preferred_element_type=jnp.float32
        ).astype(jnp.bfloat16)
        place = 0
        for index, (target, count) in enumerate(zip(targets, given)):
            write = pltpu.make_async_copy(
                out.at[pl.ds(place, count), part],
                target.at[:, part],
                out_sems.at[n * len(given) + index],
            )
            write.start()
            writes.append(write)
            place += count
    for write in writes:
        write.wait()


def expert_call(pieces, given, weights, kept, after=()):
    taken = tuple(p.shape[0] for p in pieces)
    total, width = sum(taken), pieces[0].shape[1]
    hidden = weights[2].shape[-2]
    anywhere = pl.BlockSpec(memory_space=pl.ANY)
    near = pl.BlockSpec(memory_space=pltpu.VMEM)
    outs = [jax.ShapeDtypeStruct((count, width), jnp.bfloat16) for count in given]
    scratch = [
        pltpu.VMEM((total, width), jnp.bfloat16),
        pltpu.VMEM((total, hidden), jnp.float32),
        pltpu.VMEM((total, hidden), jnp.float32),
        pltpu.VMEM((total, width), jnp.bfloat16),
        pltpu.SemaphoreType.DMA((len(taken) * DEEP,)),
        pltpu.SemaphoreType.DMA((len(given) * WIDE,)),
    ]
    if kept:
        weights = [pltpu.with_memory_space_constraint(w, pltpu.VMEM) for w in weights]
    else:
        weights = [pltpu.with_memory_space_constraint(w, pltpu.HBM) for w in weights]
        outs += [pltpu.VMEM(w.shape[1:], w.dtype) for w in weights]
        scratch.append(pltpu.SemaphoreType.DMA((2 * DEEP + WIDE,)))
    results = pl.pallas_call(
        functools.partial(expert_kernel, taken, given, kept, len(after)),
        out_shape=tuple(outs),
        in_specs=[anywhere] * len(taken)
        + [near if kept else anywhere] * 3
        + [anywhere] * len(after),
        out_specs=(anywhere,) * len(given) + (near,) * (len(outs) - len(given)),
        scratch_shapes=scratch,
        compiler_params=pltpu.CompilerParams(vmem_limit_bytes=EXPERT_VMEM),
        cost_estimate=pl.CostEstimate(flops=1000000, bytes_accessed=100000, transcendentals=0),
        name="expert_rows" if kept else "expert_rows_first",
    )(*pieces, *weights, *after)
    return results[: len(given)], results[len(given) :]


def lay_kernel(count, *refs):
    pieces, outs, sems = refs[:count], refs[-1 - count // 2 : -1], refs[-1]
    copies = []
    for index, piece in enumerate(pieces):
        rows = piece.shape[0]
        target = outs[index // 2].at[pl.ds(index % 2 * rows, rows)]
        copies.append(pltpu.make_async_copy(piece, target, sems.at[index]))
    for copy in copies:
        copy.start()
    for copy in copies:
        copy.wait()


def lay(pieces, after):
    anywhere = pl.BlockSpec(memory_space=pl.ANY)
    rows, width = pieces[0].shape
    shape = jax.ShapeDtypeStruct((2 * rows, width), pieces[0].dtype)
    return pl.pallas_call(
        functools.partial(lay_kernel, len(pieces)),
        out_shape=(shape,) * (len(pieces) // 2),
        in_specs=[anywhere] * (len(pieces) + len(after)),
        out_specs=(anywhere,) * (len(pieces) // 2),
        scratch_shapes=[pltpu.SemaphoreType.DMA((len(pieces),))],
        compiler_params=pltpu.CompilerParams(vmem_limit_bytes=1024 * 1024),
        cost_estimate=pl.CostEstimate(flops=1000, bytes_accessed=1000, transcendentals=0),
        name="lay_rows",
    )(*pieces, *after)


def attend_kernel(
    lengths, queries, new_keys, new_values, cache_k, cache_v, out_proj, mine, theirs, near_lengths, near_queries, near_keys, near_values, keys, values, heads, weights, sums, sems, out_sems
):
    count, length, _ = cache_k.shape
    share = mine.shape[2]
    width = queries.shape[1]
    group = width // HD
    blocks = count // BLOCK
    copies = []
    small = []
    for index, (source, target) in enumerate(
        (
            (lengths, near_lengths),
            (queries, near_queries),
            (new_keys, near_keys),
            (new_values, near_values),
        )
    ):
        small.append(pltpu.make_async_copy(source, target, sems.at[2 * blocks + PARTS + index]))
        small[-1].start()
    for g in range(blocks):
        part = pl.ds(g * BLOCK, BLOCK)
        copies.append(
            (
                pltpu.make_async_copy(cache_k.at[part], keys.at[part], sems.at[2 * g]),
                pltpu.make_async_copy(cache_v.at[part], values.at[part], sems.at[2 * g + 1]),
            )
        )
    rows = width // PARTS
    last = []
    for k in range(PARTS):
        part = pl.ds(k * rows, rows)
        last.append(
            pltpu.make_async_copy(out_proj.at[part], weights.at[part], sems.at[2 * blocks + k])
        )
    copies.append(tuple(last))
    for pair in copies:
        for copy in pair:
            copy.start()

    factor = 1.0 / math.sqrt(HD)
    lines = 8
    position = lax.broadcasted_iota(jnp.int32, (BLOCK, lines, length), 2)
    turn = lax.broadcasted_iota(jnp.int32, (BLOCK, lines, 1), 0)
    for copy in small:
        copy.wait()
    all_queries = near_queries[...].astype(jnp.float32)
    all_keys = near_keys[...].astype(jnp.float32)
    all_values = near_values[...].astype(jnp.float32)
    outs = []
    for g in range(blocks):
        rows = slice(g * BLOCK, (g + 1) * BLOCK)
        heads_in = [all_queries[rows, h * HD : (h + 1) * HD][:, None, :] for h in range(group)]
        empty = jnp.zeros((BLOCK, lines - group, HD), jnp.float32)
        query = jnp.concatenate(heads_in + [empty], axis=1)
        fresh_key = all_keys[rows][:, None, :]
        fresh_value = all_values[rows][:, None, :]
        used = jnp.zeros((BLOCK, lines, 1), jnp.int32)
        for r in range(BLOCK):
            used = jnp.where(turn == r, near_lengths[g * BLOCK + r], used)
        itself = jnp.sum(query * fresh_key, axis=2, keepdims=True) * factor
        for copy in copies[g]:
            copy.wait()
        scores = (
            jnp.einsum(
                "rhd,rld->rhl",
                query.astype(jnp.bfloat16),
                keys[rows],
                preferred_element_type=jnp.float32,
            )
            * factor
        )
        masked = jnp.where(position < used, scores, -jnp.inf)
        highest = jnp.maximum(jnp.max(masked, axis=2, keepdims=True), itself)
        spread = jnp.exp(masked - highest)
        own_exp = jnp.exp(itself - highest)
        inverse = 1.0 / (jnp.sum(spread, axis=2, keepdims=True) + own_exp)
        probs = (spread * inverse).astype(jnp.bfloat16)
        own_prob = (own_exp * inverse).astype(jnp.bfloat16).astype(jnp.float32)
        mixed = jnp.einsum(
            "rhl,rld->rhd", probs, values[rows], preferred_element_type=jnp.float32
        )
        mixed = mixed + own_prob * fresh_value
        outs.append(jnp.concatenate([mixed[:, h, :] for h in range(group)], axis=1))
        if g % 2 == 1:
            heads[pl.ds((g - 1) * BLOCK, 2 * BLOCK), :] = jnp.concatenate(
                outs[-2:], axis=0
            ).astype(jnp.bfloat16)

    for copy in copies[-1]:
        copy.wait()
    left = heads[...]
    chip_here, core_here = lax.axis_index("x"), lax.axis_index("c")
    writes = []
    for side, (core, target) in enumerate(((1 - core_here, theirs), (core_here, mine))):
        for k in range(SIDE):
            chip = lax.rem(chip_here + k, SIDE)
            part = pl.ds(pl.multiple_of((chip * 2 + core) * share, share), share)
            place = side * SIDE + k
            sums[place] = jnp.dot(
                left, weights[:, part], preferred_element_type=jnp.float32
            ).astype(jnp.bfloat16)
            writes.append(
                pltpu.make_async_copy(sums.at[place], target.at[k], out_sems.at[place])
            )
            writes[-1].start()
    for write in writes:
        write.wait()


def attend(queries, new_keys, new_values, cache_k, cache_v, lengths, out_proj):
    count, width = queries.shape
    length = cache_k.shape[1]
    share = out_proj.shape[1] // (2 * SIDE)
    shape = jax.ShapeDtypeStruct((SIDE, count, share), jnp.bfloat16)
    anywhere = pl.BlockSpec(memory_space=pl.ANY)
    return pl.pallas_call(
        attend_kernel,
        out_shape=(shape, shape),
        in_specs=[anywhere] * 7,
        out_specs=(anywhere, anywhere),
        scratch_shapes=[
            pltpu.SMEM(lengths.shape, jnp.int32),
            pltpu.VMEM(queries.shape, jnp.bfloat16),
            pltpu.VMEM(new_keys.shape, jnp.bfloat16),
            pltpu.VMEM(new_values.shape, jnp.bfloat16),
            pltpu.VMEM(cache_k.shape, jnp.bfloat16),
            pltpu.VMEM(cache_v.shape, jnp.bfloat16),
            pltpu.VMEM((count, width), jnp.bfloat16),
            pltpu.VMEM(out_proj.shape, jnp.bfloat16),
            pltpu.VMEM((2 * SIDE, count, share), jnp.bfloat16),
            pltpu.SemaphoreType.DMA((2 * count // BLOCK + PARTS + 4,)),
            pltpu.SemaphoreType.DMA((2 * SIDE,)),
        ],
        compiler_params=pltpu.CompilerParams(vmem_limit_bytes=VMEM),
        cost_estimate=pl.CostEstimate(
            flops=2 * count * width * out_proj.shape[1],
            bytes_accessed=4 * count * length * HD,
            transcendentals=0,
        ),
        name="attend_rows",
    )(lengths, queries, new_keys, new_values, cache_k, cache_v, out_proj)


def slot_codes(route_ids, experts, capacity):
    routes = route_ids.reshape(MICRO, MB, TOP)
    onehot = (routes[..., None] == jnp.arange(experts, dtype=jnp.int32)).astype(jnp.int32)
    flat = onehot.reshape(MICRO, MB * TOP, experts)
    before = jnp.cumsum(flat, axis=1) - flat
    slots = jnp.sum(before * flat, axis=-1).reshape(MICRO, MB, TOP)
    batch = jnp.arange(MICRO, dtype=jnp.int32)[:, None, None]
    return ((routes * MICRO + batch) * capacity + slots).reshape(MICRO * MB, TOP)


def body(
    resid,
    queries,
    new_keys,
    new_values,
    cache_k,
    cache_v,
    lengths,
    out_proj,
    norm_gain,
    router,
    route_ids,
    w_gate,
    w_up,
    w_down,
):
    count, model_width = resid.shape
    experts = router.shape[1]
    capacity = 4 * MB // experts
    slots = MICRO * capacity
    share = model_width // experts
    mine = lax.axis_index(EXPERT_AXES)

    own, others = attend(queries, new_keys, new_values, cache_k, cache_v, lengths, out_proj)
    arrived = lax.ppermute(others, "c", [(0, 1), (1, 0)])
    sums = [add(own[k], arrived[k]) for k in range(SIDE)]
    sums = [sums[0]] + [shift(sums[k], "x", k) for k in range(1, SIDE)]

    route_ids, _ = lax.optimization_barrier((route_ids, own))
    codes = slot_codes(route_ids, experts, capacity)
    places = jnp.arange(experts * slots, dtype=jnp.int32)[:, None]
    dispatch = ((codes[None, :, 0] == places) | (codes[None, :, 1] == places)).astype(jnp.bfloat16)
    slot = jnp.arange(slots, dtype=jnp.int32)[:, None]
    hits = [(c // slots == mine)[None] & (c % slots == slot) for c in (codes[:, 0], codes[:, 1])]
    own_dispatch = (hits[0] | hits[1]).astype(jnp.bfloat16)
    expert_ids = jnp.arange(experts, dtype=jnp.int32)
    match = jnp.sum((route_ids[:, :, None] == expert_ids).astype(jnp.bfloat16), axis=1)
    both = jnp.dot(own_dispatch, match, preferred_element_type=jnp.float32)
    own_mask = (expert_ids == mine)[None, :]

    state = lax.dynamic_slice_in_dim(resid, mine * share, share, 1).astype(jnp.float32)
    for one in sums:
        state = state + one.astype(jnp.float32)
    sent = jnp.dot(dispatch, state.astype(jnp.bfloat16), preferred_element_type=jnp.float32)
    sent = sent.astype(jnp.bfloat16).reshape(experts, slots, share)
    rows = lax.all_to_all(sent, EXPERT_AXES, 0, 0, tiled=True).astype(jnp.float32)
    mean_square = jnp.sum(rows * rows, axis=(0, 2)) / model_width
    gain = norm_gain.astype(jnp.float32).reshape(experts, 1, share)
    normed = (rows * lax.rsqrt(mean_square + epsilon)[None, :, None] * gain).astype(jnp.bfloat16)
    normed = normed.transpose(1, 0, 2).reshape(slots, model_width)

    logits = jnp.dot(normed, router, preferred_element_type=jnp.float32)
    own_logit = jnp.sum(jnp.where(own_mask, logits, 0.0), axis=1)
    other_logit = jnp.sum(jnp.where(own_mask, 0.0, logits * both), axis=1)
    gates = (1.0 / (1.0 + jnp.exp(other_logit - own_logit))).astype(jnp.bfloat16)

    def step(pair, turn):
        return ring(pair[0], "y", turn), ring(pair[1], "z", turn)

    def turn_over(pair, turn):
        return swap(pair[0], "z", turn), swap(pair[1], "y", turn)

    def join(left, right):
        return add(left[0], right[0]), add(left[1], right[1])

    start = (normed[:capacity], normed[capacity:])
    partner = turn_over(start, 0)
    near = tuple(jnp.concatenate(both, axis=0) for both in zip(start, partner))
    apart = turn_over(near, 1)
    whole = (4 * capacity,) * 2

    def pieces(one, two):
        return one[0], two[0], one[1], two[1]

    behind = step(near, 0), step(apart, 0)
    far = step(behind[0], 0), step(behind[1], 0)
    own_part, kept = expert_call(pieces(near, apart), whole, (w_gate, w_up, w_down), False)
    ahead = step(lay(pieces(near, apart), far[0]), 1)
    far_part, _ = expert_call(pieces(*far), whole, kept, True)
    far_sum = step(far_part, 1)
    behind_part, _ = expert_call(pieces(*behind), whole, kept, True, far_part)
    ahead_part, _ = expert_call(ahead, whole, kept, True)
    from_behind = step(ahead_part, 0)
    from_ahead = step(join(far_sum, behind_part), 1)

    def collect(side, axis):
        value = own_part[side].astype(jnp.float32) + from_behind[side].astype(jnp.float32)
        value = value + from_ahead[side].astype(jnp.float32)
        value = value.reshape(SIDE, capacity, model_width)
        sent = value[1:].astype(jnp.bfloat16)
        total = value[0] + swap(sent[0], axis, 0).astype(jnp.float32)
        total = total + swap(sent[1], axis, 1).astype(jnp.float32)
        return total + shift(sent[2], axis, 2).astype(jnp.float32)

    expert_out = jnp.concatenate([collect(0, "z"), collect(1, "y")], axis=0)

    weighted = (expert_out * gates.astype(jnp.float32)[:, None]).astype(jnp.bfloat16)
    weighted = weighted.reshape(slots, experts, share).transpose(1, 0, 2)
    back = lax.all_to_all(weighted, EXPERT_AXES, 0, 0, tiled=True)
    moe = lax.dot_general(
        dispatch,
        back.reshape(experts * slots, share),
        (((0,), (0,)), ((), ())),
        preferred_element_type=jnp.float32,
    )
    return (state + moe).astype(jnp.bfloat16)


def solution(mesh):
    fine = Mesh(mesh.devices.reshape(SIDE, SIDE, SIDE, 2), ("y", "z", "x", "c"))
    attn = ("y", "z")
    placed = (
        P(attn, None),
        P(attn, EXPERT_AXES),
        P(attn, EXPERT_AXES),
        P(attn, EXPERT_AXES),
        P(attn, None, EXPERT_AXES),
        P(attn, None, EXPERT_AXES),
        P(attn),
        P(EXPERT_AXES, None),
        P(),
        P(),
        P(attn, None),
        P(EXPERT_AXES, None, attn),
        P(EXPERT_AXES, None, attn),
        P(EXPERT_AXES, attn, None),
    )
    return jax.shard_map(
        body, mesh=fine, in_specs=placed, out_specs=P(attn, EXPERT_AXES), check_vma=False
    )
```
